512 devices in a mesh: chaos: 32 (over y, x, core), sx: 4 (over z_hi), sy: 4 (over z_lo).
Axes of the slice: x: 4, y: 4, z: 16 (z_hi: 4, z_lo: 4; z = z_hi * 4 + z_lo), core: 2. Of those that a mesh axis runs over, the one named last changes fastest.
Arguments:
- right_side: float32 [512, 128, 512], P('chaos', 'sx', 'sy'), may hold values from -6 to 6
- mean_coef: float32 [128, 512], P('sx', 'sy'), may hold values from 0.2 to 2
- mode_coef: float32 [10, 128, 512], P(None, 'sx', 'sy'), may hold values from -0.6 to 0.6
- coupling: bfloat16 [10, 2, 8, 4096], replicated, may hold values from -0.375 to 0.375
- offsets: int32 [10, 2], replicated, may hold values from 0 to 7
- lower_bound: float32 [1], replicated, may hold values from 0.5 to 3
- upper_bound: float32 [1], replicated, may hold values from 10 to 30
Outputs:
- solution: float32 [512, 128, 512], P('chaos', 'sx', 'sy')
The draws below stay inside these ranges and needn't reach their ends.
Inputs may be any that keep to these rules, and one draw needn't show every extreme that they name: Block diagonal offsets; a mode may repeat an offset, and repeated diagonals add.
All inputs are finite; a program needn't handle non-finite values.
Results may differ from the reference program's by a relative error of at most 0.0003.
Values sent between devices are 32-bit elements; how exact they have to be, the bound alone decides.
No kernel may reach another device: no remote copies, remote signals or barrier semaphores. Data moves between devices by JAX's collectives and lax.ppermute only.
A program may use at most 64 MiB of HBM per device.

```python
import math
import jax
import jax.numpy as jnp
from jax import lax

MODES = 10
BLOCK = 64
NBLOCKS = 8
DIAGS = 2
STEPS = 2
TERMS = 512
NX = 128
NY = 256


def plant(array, stream_key, smallest, top_value):
    dims = array.shape
    index_at = [jax.random.randint(jax.random.fold_in(stream_key, axis), (), 0, dims[axis]) for axis in range(len(dims))]
    array = array.at[tuple(index_at)].set(smallest)
    longest = dims.index(max(dims))
    index_at[longest] = (index_at[longest] + 1) % dims[longest]
    return array.at[tuple(index_at)].set(top_value)


def level_of(rng, dims, split, smallest, largest):
    def one(dim, parts):
        steps = jax.random.uniform(jax.random.fold_in(jax.random.fold_in(rng, 6), dim), (parts,), jnp.float32, smallest / len(split), largest / len(split))
        return jnp.repeat(jnp.exp(steps), dims[dim] // parts).reshape((-1,) + (1,) * (len(dims) - dim - 1))

    factor_of = one(*split[0])
    for cut in split[1:]:
        factor_of = factor_of * one(*cut)
    return factor_of


def scatter_about(own_key, shape, deviation, most, shards=(), held_as=jnp.bfloat16):
    result = jax.random.normal(own_key, shape, jnp.float32) * deviation
    if len(shards) > 0:
        result = level_of(own_key, shape, shards, -0.22, 0.18) * result
    return jnp.clip(result, min=-most, max=most).astype(held_as)


def setup_inputs(seed: int = 0) -> dict:
    arg_keys = jax.random.split(jax.random.key(seed), 8)
    return {
        "right_side": scatter_about(arg_keys[0], (TERMS, NX, 2 * NY), 1.0, 6.0, ((0, 32), (1, 4), (2, 4)), jnp.float32),
        "mean_coef": jnp.clip(jnp.exp(math.log(2.0) - 2.3025851 * jax.random.uniform(arg_keys[1], (NX, 2 * NY), jnp.float32) ** level_of(arg_keys[1], (NX, 2 * NY), ((0, 4), (1, 4)), -0.2, 0.2)), 0.2, 2.0),
        "mode_coef": scatter_about(arg_keys[2], (MODES, NX, 2 * NY), 0.1, 0.6, ((1, 4), (2, 4)), jnp.float32),
        "coupling": scatter_about(arg_keys[3], (MODES, DIAGS, NBLOCKS, BLOCK * BLOCK), (4 * BLOCK) ** -0.5, 0.375),
        "offsets": plant(jax.random.randint(arg_keys[4], (MODES, DIAGS), 0, NBLOCKS), jax.random.fold_in(arg_keys[4], 1), 0, NBLOCKS - 1).astype(jnp.int32),
        "lower_bound": jnp.clip(jax.random.uniform(arg_keys[5], (1,), jnp.float32, 0.5, 3.0), 0.5, 3.0),
        "upper_bound": jnp.clip(jax.random.uniform(arg_keys[6], (1,), jnp.float32, 10.0, 30.0), 10.0, 30.0),
    }


def plane_view(values):
    return values.reshape(values.shape[:-1] + (values.shape[-1] // 2, 2))


def face_weights(coefficient):
    return [
        (coefficient + jnp.roll(coefficient, 1, axis=0)) * 0.5,
        (coefficient + jnp.roll(coefficient, -1, axis=0)) * 0.5,
        (coefficient + jnp.roll(coefficient, 1, axis=1)) * 0.5,
        (coefficient + jnp.roll(coefficient, -1, axis=1)) * 0.5,
        (coefficient + coefficient[..., ::-1]) * 0.5,
    ]


def apply_mode(source_field, coefficient):
    weights = face_weights(coefficient)
    others = [
        jnp.roll(source_field, 1, axis=1),
        jnp.roll(source_field, -1, axis=1),
        jnp.roll(source_field, 1, axis=2),
        jnp.roll(source_field, -1, axis=2),
        source_field[..., ::-1],
    ]
    totals = weights[0][None] * (source_field - others[0])
    for face in range(1, 5):
        totals = totals + weights[face][None] * (source_field - others[face])
    return totals


def apply_operator(source_flat, mean_coef, mode_coef, coupling, offsets):
    source_field = plane_view(source_flat)
    local_part = source_field + apply_mode(source_field, plane_view(mean_coef))

    def per_mode(mixed, inputs):
        coefficient, blocks, shifts = inputs
        diffused = apply_mode(source_field, plane_view(coefficient)).reshape(NBLOCKS, BLOCK, -1)
        for diag_index in range(DIAGS):
            matrix = blocks[diag_index].reshape(NBLOCKS, BLOCK, BLOCK).astype(jnp.float32)
            shift_by = shifts[diag_index]
            mixed = mixed + jnp.einsum("dab,dbc->dac", matrix, jnp.roll(diffused, -shift_by, axis=0),
                                       precision=lax.Precision.HIGHEST)
            mixed = mixed + jnp.roll(jnp.einsum("dba,dbc->dac", matrix, diffused,
                                                precision=lax.Precision.HIGHEST), shift_by, axis=0)
        return mixed, None

    start = jnp.zeros((NBLOCKS, BLOCK, NX * 2 * NY), jnp.float32)
    mixed, unused = lax.scan(per_mode, start, (mode_coef, coupling, offsets))
    return local_part.reshape(source_flat.shape) + mixed.reshape(source_flat.shape)


def reference(right_side, mean_coef, mode_coef, coupling, offsets, lower_bound, upper_bound):
    lower_end = lower_bound[0]
    upper_end = upper_bound[0]
    middle = (upper_end + lower_end) * 0.5
    half_width = (upper_end - lower_end) * 0.5
    spread_ratio = middle / half_width
    factor_now = 1.0 / spread_ratio
    direction = right_side / middle
    solution = direction
    residual = right_side
    for iteration in range(1, STEPS):
        residual = residual - apply_operator(direction, mean_coef, mode_coef, coupling, offsets)
        factor_next = 1.0 / (2.0 * spread_ratio - factor_now)
        direction = factor_next * factor_now * direction + (2.0 * factor_next / half_width) * residual
        solution = solution + direction
        factor_now = factor_next
    return solution
```

```python
import functools

import jax
import jax.numpy as jnp
from jax import lax
from jax.experimental import pallas as pl
from jax.experimental.pallas import tpu as pltpu
from jax.sharding import PartitionSpec as P

f32 = jnp.float32
bf16 = jnp.bfloat16
MODES = 10


def block_device(bi, bj):
    high, core = ((0, 0), (1, 0), (1, 1), (0, 1))[bi]
    low, y = (0, bj) if bj < 4 else (1, 7 - bj)
    return y * 8 + (2 * high + low) * 2 + core


def device_block(index):
    core, x, y = index % 2, (index // 2) % 4, index // 8
    bi = jnp.where(x < 2, 3 * core, 1 + core)
    bj = jnp.where(x % 2 == 0, y, 7 - y)
    return bi, bj


def lanes():
    return lax.broadcasted_iota(jnp.int32, (8, 128), 1)


def roll(value, shift):
    if isinstance(shift, int):
        shift = shift % 128
        if shift == 0:
            return value
    return pltpu.roll(value, shift, 1)


def swap_chunks(rows, lane):
    rows = list(rows)
    for step in (1, 2, 4):
        low = (lane // 16) & step == 0
        for i in range(8):
            if i & step == 0:
                a, b = rows[i], rows[i + step]
                rows[i] = jnp.where(low, a, roll(b, 16 * step))
                rows[i + step] = jnp.where(low, roll(a, -16 * step), b)
    return rows


def pack_kernel(field, slots):
    lane = lanes()
    column = lane % 16
    for bi in range(4):
        blocks, above, below = [], [], []
        for h in range(2):
            terms = slice(8 * h, 8 * h + 8)
            blocks.append(swap_chunks([field[terms, 8 * bi + i, :] for i in range(8)], lane))
            above.append(field[terms, (8 * bi - 1) % 32, :])
            below.append(field[terms, (8 * bi + 8) % 32, :])
        for bj in range(8):
            at = block_device(bi, bj)
            units = []
            for h in range(2):
                slots[at, 8 * h : 8 * h + 8, :] = blocks[h][bj]
                side = jnp.where(column >= 8, blocks[h][(bj - 1) % 8], blocks[h][(bj + 1) % 8])
                units.append(roll(side, 2 + 4 * h))
            row = jnp.where(column < 4, units[0], units[1])
            row = jnp.where(lane % 32 < 8, row, roll(row, -8))
            row = jnp.where(lane % 64 < 16, row, roll(row, -16))
            row = jnp.where(lane < 32, row, roll(row, -32))
            for h in range(2):
                start = 64 + 32 * h
                next_row = roll(below[h], start - 16 * bj)
                row = jnp.where((lane >= start) & (lane < start + 16), next_row, row)
                last_row = roll(above[h], start + 16 - 16 * bj)
                row = jnp.where((lane >= start + 16) & (lane < start + 32), last_row, row)
            slots[at, 16:24, :] = row


def spread_units(row, lane):
    row = jnp.where(lane < 32, row, roll(row, 32))
    row = jnp.where(lane % 64 < 16, row, roll(row, 16))
    return jnp.where(lane % 32 < 8, row, roll(row, 8))


def prepare_kernel(coupling, offsets, mean_coef, mode_coef, weights, coefs, pairs, tile, parts):
    lane = lanes()
    first = lane < 64
    bi, bj = device_block(lax.axis_index("chaos"))
    tile[0] = mean_coef[...]
    tile[1 : MODES + 1] = mode_coef[...]
    tile[MODES + 1 :] = jnp.zeros((15 - MODES, 32, 128), f32)
    for h in range(2):
        terms = slice(8 * h, 8 * h + 8)
        blocks = swap_chunks([tile[terms, 8 * bi + i, :] for i in range(8)], lane)
        for j in range(8):
            parts[j] = blocks[j]
        coefs[8 * h : 8 * h + 8, :] = parts[bj]
        above = tile[terms, lax.rem(8 * bi + 31, 32), :]
        below = tile[terms, lax.rem(8 * bi + 8, 32), :]
        beside = jnp.where(
            lane < 64,
            pltpu.roll(above, lax.rem(128 - 16 * bj, 128), 1),
            pltpu.roll(below, lax.rem(240 - 16 * bj, 128), 1),
        )
        coefs[16 + 8 * h : 24 + 8 * h, :] = beside
        sides = jnp.where(
            lane % 16 < 8, roll(parts[lax.rem(bj + 7, 8)], -14), roll(parts[lax.rem(bj + 1, 8)], 14)
        )
        coefs[32 + 8 * h : 40 + 8 * h, :] = sides
    out_row = lax.broadcasted_iota(jnp.int32, (64, 128), 0)
    out_col = lax.broadcasted_iota(jnp.int32, (64, 128), 1)
    pick = jnp.where(out_col % 64 == out_row, 1.0, 0.0).astype(bf16)
    wide = lax.broadcasted_iota(jnp.int32, (64, 128), 1) < 64

    def one_mode(k, carry):
        for m in range(32):
            both = coupling[pl.ds(pl.multiple_of(16 * k, 16), 16), 128 * m : 128 * m + 128].astype(f32)
            one, two = both[:8], both[8:]
            pairs[pl.ds(2 * m, 8, 64), :] = jnp.where(first, one, roll(two, 64))
            pairs[pl.ds(2 * m + 1, 8, 64), :] = jnp.where(first, roll(one, 64), two)
        shift_one, shift_two = offsets[2 * k], offsets[2 * k + 1]
        for d in range(8):
            weights[d, k, :, 0:128] = pairs[64 * d : 64 * d + 64, :].astype(bf16)
            from_one = lax.rem(d + 8 - shift_one, 8)
            from_two = lax.rem(d + 8 - shift_two, 8)
            one = pairs[pl.ds(pl.multiple_of(64 * from_one, 64), 64), :]
            two = pairs[pl.ds(pl.multiple_of(64 * from_two, 64), 64), :]
            stack = jnp.concatenate([jnp.where(wide, one, 0.0), jnp.where(wide, 0.0, two)], axis=0)
            turned = lax.dot_general(
                pick, stack.astype(bf16), (((1,), (1,)), ((), ())), preferred_element_type=f32
            )
            weights[d, k, :, 128:256] = turned.astype(bf16)
        return carry

    lax.fori_loop(0, MODES, one_mode, 0)


def edges_kernel(slots, coefs, rows_out, columns_out):
    lane = lanes()
    bi, bj = device_block(lax.axis_index("chaos"))
    row_shift = jnp.where(bi == 0, 0, 16)
    column_shift = jnp.where(bj == 0, 0, 114)
    for r in range(8):
        row = jnp.zeros((8, 128), f32)
        column = jnp.zeros((8, 128), f32)
        for q in range(8):
            at, h = 4 * q + r // 2, r % 2
            block = slots[at, 8 * h : 8 * h + 8, :]
            row = jnp.where(lane // 16 == q, pltpu.roll(block, lax.rem(row_shift + 16 * q, 128), 1), row)
            column = jnp.where(
                (lane % 16) // 2 == q, pltpu.roll(block, lax.rem(column_shift + 2 * q, 128), 1), column
            )
        rows_out[8 * r : 8 * r + 8, :] = row
        columns_out[8 * r : 8 * r + 8, :] = column
    rows_out[64:80, :] = coefs[0:16, :]
    columns_out[64:80, :] = coefs[0:16, :]


def operator_kernel(slots, coefs, rows_in, columns_in, weights, offsets, out, faces, spread):
    lane = lanes()
    column = lane % 16
    even = lane % 2 == 0
    bi, bj = device_block(lax.axis_index("chaos"))
    top, bottom = lane < 16, lane >= 112
    left, right = column < 2, column >= 14
    row_edge = ((bi == 0) & top) | ((bi == 3) & bottom)
    column_edge = ((bj == 0) & left) | ((bj == 7) & right)
    row_target = jnp.where(bi == 0, 128, 240)
    column_target = jnp.where(bj == 0, 128, 142)

    def neighbours(block, beside, sides):
        return (
            jnp.where(top, beside, roll(block, 16)),
            jnp.where(bottom, beside, roll(block, -16)),
            jnp.where(left, sides, roll(block, 2)),
            jnp.where(right, sides, roll(block, -2)),
            jnp.where(even, roll(block, -1), roll(block, 1)),
        )

    row_coef = jnp.where(bi == 0, 16, 112)
    column_coef = jnp.where(bj == 0, 114, 14)
    for h in range(2):
        terms = slice(8 * h, 8 * h + 8)
        edge_terms = slice(64 + 8 * h, 72 + 8 * h)
        center = coefs[terms, :]
        beside = jnp.where(
            row_edge, pltpu.roll(rows_in[edge_terms, :], row_coef, 1), coefs[16 + 8 * h : 24 + 8 * h, :]
        )
        sides = jnp.where(
            column_edge, pltpu.roll(columns_in[edge_terms, :], column_coef, 1), coefs[32 + 8 * h : 40 + 8 * h, :]
        )
        for face, other in enumerate(neighbours(center, beside, sides)):
            faces[face, terms, :] = (center + other) * 0.5

    def one_slot(s, carry):
        q, r = s // 4, s % 4
        units = slots[s, 16:24, :]
        opened = spread_units(units, lane)
        halves = []
        for h in range(2):
            block = slots[s, 8 * h : 8 * h + 8, :]
            edge_terms = pl.ds(pl.multiple_of(16 * r + 8 * h, 8), 8)
            beside = roll(units, -(80 + 32 * h))
            beside = jnp.where(
                row_edge, pltpu.roll(rows_in[edge_terms, :], lax.rem(row_target - 16 * q, 128), 1), beside
            )
            sides = jnp.where(column < 8, roll(opened, -(16 + 4 * h)), roll(opened, 12 - 4 * h))
            sides = jnp.where(
                column_edge,
                pltpu.roll(columns_in[edge_terms, :], lax.rem(column_target - 2 * q, 128), 1),
                sides,
            )
            others = neighbours(block, beside, sides)
            halves.append((block, [block - other for other in others]))

        def diffuse(k):
            sums = []
            for block, differences in halves:
                total = faces[0, k : k + 1, :] * differences[0]
                for face in range(1, 5):
                    total = total + faces[face, k : k + 1, :] * differences[face]
                sums.append(total)
            return sums

        for h, total in enumerate(diffuse(0)):
            out[s, 8 * h : 8 * h + 8, :] = halves[h][0] + total
        for k in range(MODES):
            total = jnp.concatenate(diffuse(k + 1), axis=0)
            high = total.astype(bf16)
            low = (total - high.astype(f32)).astype(bf16)
            at = pl.ds(pl.multiple_of(512 * k + 16 * s, 16), 16)
            spread[at, 0:128] = high
            spread[at, 128:256] = low
        return carry

    lax.fori_loop(0, 32, one_slot, 0)

    def one_block(d, carry):
        total = jnp.zeros((64, 256), f32)
        for k in range(MODES):
            shift_one, shift_two = offsets[2 * k], offsets[2 * k + 1]
            gathered = []
            for at in (d + shift_one, d + shift_two, d + 8 - shift_one, d + 8 - shift_two):
                start = pl.multiple_of(512 * k + 64 * lax.rem(at, 8), 64)
                gathered.append(spread[pl.ds(start, 64), :])
            total = total + jnp.dot(
                weights[d, k], jnp.concatenate(gathered, axis=0), preferred_element_type=f32
            )
        mixed = total[:, :128] + total[:, 128:]
        for part in range(4):
            out[4 * d + part] = out[4 * d + part] + mixed[16 * part : 16 * part + 16]
        return carry

    lax.fori_loop(0, 8, one_block, 0, unroll=2)


def finish_kernel(field, slots, lower_bound, upper_bound, out):
    lane = lanes()
    lower_end = jnp.full((8, 128), lower_bound[0], f32)
    upper_end = jnp.full((8, 128), upper_bound[0], f32)
    middle = (upper_end + lower_end) * 0.5
    half_width = (upper_end - lower_end) * 0.5
    spread_ratio = middle / half_width
    factor_now = 1.0 / spread_ratio
    factor_next = 1.0 / (2.0 * spread_ratio - factor_now)
    residual_scale = 2.0 * factor_next / half_width
    field_scale = (1.0 + factor_next * factor_now) / middle + residual_scale
    applied_scale = residual_scale / middle
    for bi in range(4):
        for h in range(2):
            terms = slice(8 * h, 8 * h + 8)
            rows = swap_chunks([slots[block_device(bi, bj), terms, :] for bj in range(8)], lane)
            for i in range(8):
                at = 8 * bi + i
                out[terms, at, :] = field_scale * field[terms, at, :] - applied_scale * rows[i]


def in_vmem():
    return pl.BlockSpec(memory_space=pltpu.VMEM)


def in_smem():
    return pl.BlockSpec(memory_space=pltpu.SMEM)


def call(kernel, ins, outs, scratch=(), cost=None, limit=None):
    return pl.pallas_call(
        kernel,
        out_shape=outs,
        in_specs=ins,
        out_specs=jax.tree.map(lambda _: in_vmem(), outs),
        scratch_shapes=scratch,
        cost_estimate=cost,
        compiler_params=pltpu.CompilerParams(vmem_limit_bytes=limit or 32 * 2**20),
        name=kernel.__name__,
    )


def per_device(right_side, mean_coef, mode_coef, coupling, offsets, lower_bound, upper_bound):
    shape = jax.ShapeDtypeStruct
    slots = call(pack_kernel, [in_vmem()], shape((32, 24, 128), f32))(right_side)
    held = lax.all_to_all(slots, "chaos", 0, 0, tiled=True)
    flat_offsets = offsets.reshape(2 * MODES)
    weights, coefs = call(
        prepare_kernel,
        [in_vmem(), in_smem(), in_vmem(), in_vmem()],
        (shape((8, MODES, 64, 256), bf16), shape((48, 128), f32)),
        [pltpu.VMEM((512, 128), f32), pltpu.VMEM((16, 32, 128), f32), pltpu.VMEM((8, 8, 128), f32)],
        pl.CostEstimate(flops=2**27, bytes_accessed=2**22, transcendentals=0),
    )(coupling.reshape(16 * MODES, 4096), flat_offsets, mean_coef, mode_coef)
    rows_out, columns_out = call(
        edges_kernel, [in_vmem()] * 2, (shape((80, 128), f32), shape((80, 128), f32))
    )(held, coefs)

    def index(device, sx, sy):
        return (device * 4 + sx % 4) * 4 + sy % 4

    row_pairs, column_pairs = [], []
    for sx in range(4):
        for sy in range(4):
            for bj in range(8):
                low, high = block_device(0, bj), block_device(3, bj)
                row_pairs.append((index(high, sx, sy), index(low, sx + 1, sy)))
                row_pairs.append((index(low, sx, sy), index(high, sx - 1, sy)))
            for bi in range(4):
                low, high = block_device(bi, 0), block_device(bi, 7)
                column_pairs.append((index(high, sx, sy), index(low, sx, sy + 1)))
                column_pairs.append((index(low, sx, sy), index(high, sx, sy - 1)))
    axes = ("chaos", "sx", "sy")
    rows_in = lax.ppermute(rows_out, axes, row_pairs)
    columns_in = lax.ppermute(columns_out, axes, column_pairs)
    applied = call(
        operator_kernel,
        [in_vmem()] * 5 + [in_smem()],
        shape((32, 16, 128), f32),
        [pltpu.VMEM((5, 16, 128), f32), pltpu.VMEM((512 * MODES, 256), bf16)],
    )(held, coefs, rows_in, columns_in, weights, flat_offsets)
    returned = lax.all_to_all(applied, "chaos", 0, 0, tiled=True)
    return call(
        finish_kernel,
        [in_vmem()] * 2 + [in_smem()] * 2,
        shape(right_side.shape, f32),
    )(right_side, returned, lower_bound, upper_bound)


def solution(mesh):
    return jax.shard_map(
        per_device,
        mesh=mesh,
        in_specs=(P("chaos", "sx", "sy"), P("sx", "sy"), P(None, "sx", "sy"), P(), P(), P(), P()),
        out_specs=P("chaos", "sx", "sy"),
        check_vma=False,
    )
```

```python
import functools

import jax
import jax.numpy as jnp
from jax import lax
from jax.experimental import pallas as pl
from jax.experimental.pallas import tpu as pltpu
from jax.sharding import PartitionSpec as P

f32 = jnp.float32
bf16 = jnp.bfloat16
MODES = 10


def block_device(bi, bj):
    core = (0, 0, 1, 1)[bi]
    outer = bi in (0, 3)
    if bj < 4:
        x, y = (0 if outer else 1), bj
    else:
        x, y = (3 if outer else 2), 7 - bj
    return y * 8 + x * 2 + core


def device_block(index):
    core, x, y = index % 2, (index // 2) % 4, index // 8
    bi = jnp.where((x == 0) | (x == 3), 3 * core, 1 + core)
    bj = jnp.where(x < 2, y, 7 - y)
    return bi, bj


def lane_numbers():
    return lax.broadcasted_iota(jnp.int32, (8, 128), 1)


def roll(value, shift):
    if isinstance(shift, int):
        shift = shift % 128
        if shift == 0:
            return value
    return pltpu.roll(value, shift, 1)


def chunk_masks(lane):
    return {step: lane & (16 * step) == 0 for step in (1, 2, 4)}


def swap_chunks(rows, low):
    rows = list(rows)
    for step in (1, 2, 4):
        for i in range(8):
            if i & step == 0:
                a, b = rows[i], rows[i + step]
                rows[i] = jnp.where(low[step], a, roll(b, 16 * step))
                rows[i + step] = jnp.where(low[step], roll(a, -16 * step), b)
    return rows


def unit_masks(lane):
    return lane & 31 < 8, lane & 63 < 16, lane < 32


def pack_kernel(source, target, field, slots, arrived, left):
    copies = [
        pltpu.make_async_copy(
            source.at[:, 8 * bi : 8 * bi + 8, :], field.at[:, 8 * bi : 8 * bi + 8, :], arrived.at[bi]
        )
        for bi in range(4)
    ]
    for copy in copies:
        copy.start()
    lane = lane_numbers()
    low = chunk_masks(lane)
    unit_first, unit_second, unit_third = unit_masks(lane)
    column = lane & 15
    upper, unit_half = column >= 8, column < 4
    next_place = [(lane >> 4) == 4 + 2 * h for h in range(2)]
    last_place = [(lane >> 4) == 5 + 2 * h for h in range(2)]
    for copy in copies:
        copy.wait()
    leaving = []
    for bi in range(4):
        blocks, above, below = [], [], []
        for h in range(2):
            terms = slice(8 * h, 8 * h + 8)
            rows = [field[terms, 8 * bi + i, :] for i in range(8)]
            blocks.append(swap_chunks(rows, low))
            above.append(field[terms, 8 * bi - 1, :] if bi > 0 else rows[0])
            below.append(field[terms, 8 * bi + 8, :] if bi < 3 else rows[7])
        for bj in range(8):
            at = block_device(bi, bj)
            units = []
            for h in range(2):
                slots[at, 8 * h : 8 * h + 8, :] = blocks[h][bj]
                side = jnp.where(upper, blocks[h][(bj - 1) % 8], blocks[h][(bj + 1) % 8])
                units.append(roll(side, 2 + 4 * h))
            row = jnp.where(unit_half, units[0], units[1])
            row = jnp.where(unit_first, row, roll(row, -8))
            row = jnp.where(unit_second, row, roll(row, -16))
            row = jnp.where(unit_third, row, roll(row, -32))
            for h in range(2):
                start = 64 + 32 * h
                row = jnp.where(next_place[h], roll(below[h], start - 16 * bj), row)
                row = jnp.where(last_place[h], roll(above[h], start + 16 - 16 * bj), row)
            slots[at, 16:24, :] = row
        for bj in range(8):
            at = block_device(bi, bj)
            leaving.append(pltpu.make_async_copy(slots.at[at], target.at[at], left.at[at]))
            leaving[-1].start()
    for copy in leaving:
        copy.wait()


def prepare_kernel(
    coupling_at, offsets, mean_at, mode_at, weights, coefs, coupling, pairs, tile, parts, arrived
):
    copies = [
        pltpu.make_async_copy(mean_at, tile.at[0], arrived.at[0]),
        pltpu.make_async_copy(mode_at, tile.at[1 : MODES + 1], arrived.at[1]),
        pltpu.make_async_copy(coupling_at, coupling, arrived.at[2]),
    ]
    for copy in copies:
        copy.start()
    tile[MODES + 1 :] = jnp.zeros((15 - MODES, 32, 128), f32)
    lane = lane_numbers()
    low = chunk_masks(lane)
    first = lane < 64
    left_half = lane & 15 < 8
    bi, bj = device_block(lax.axis_index("chaos"))
    copies[0].wait()
    copies[1].wait()
    for h in range(2):
        terms = slice(8 * h, 8 * h + 8)
        blocks = swap_chunks([tile[terms, 8 * bi + i, :] for i in range(8)], low)
        for j in range(8):
            parts[j] = blocks[j]
        coefs[8 * h : 8 * h + 8, :] = parts[bj]
        above = tile[terms, lax.rem(8 * bi + 31, 32), :]
        below = tile[terms, lax.rem(8 * bi + 8, 32), :]
        coefs[16 + 8 * h : 24 + 8 * h, :] = jnp.where(
            first,
            pltpu.roll(above, lax.rem(128 - 16 * bj, 128), 1),
            pltpu.roll(below, lax.rem(240 - 16 * bj, 128), 1),
        )
        coefs[32 + 8 * h : 40 + 8 * h, :] = jnp.where(
            left_half, roll(parts[lax.rem(bj + 7, 8)], -14), roll(parts[lax.rem(bj + 1, 8)], 14)
        )
    out_row = lax.broadcasted_iota(jnp.int32, (64, 128), 0)
    out_col = lax.broadcasted_iota(jnp.int32, (64, 128), 1)
    pick = jnp.where(out_col & 63 == out_row, 1.0, 0.0).astype(bf16)
    wide = out_col < 64
    copies[2].wait()

    def one_mode(k, carry):
        base = pl.multiple_of(512 * k, 512)
        for m in range(32):
            both = coupling[pl.ds(pl.multiple_of(16 * k, 16), 16), 128 * m : 128 * m + 128].astype(f32)
            one, two = both[:8], both[8:]
            pairs[pl.ds(base + 2 * m, 8, 64), :] = jnp.where(first, one, roll(two, 64))
            pairs[pl.ds(base + 2 * m + 1, 8, 64), :] = jnp.where(first, roll(one, 64), two)
        shift_one, shift_two = offsets[0, k], offsets[1, k]
        for d in range(8):
            weights[d, k, :, 0:128] = pairs[pl.ds(base + 64 * d, 64), :].astype(bf16)
            from_one = lax.rem(d + 8 - shift_one, 8)
            from_two = lax.rem(d + 8 - shift_two, 8)
            one = pairs[pl.ds(pl.multiple_of(base + 64 * from_one, 64), 64), :]
            two = pairs[pl.ds(pl.multiple_of(base + 64 * from_two, 64), 64), :]
            stack = jnp.concatenate([jnp.where(wide, one, 0.0), jnp.where(wide, 0.0, two)], axis=0)
            turned = lax.dot_general(
                pick, stack.astype(bf16), (((1,), (1,)), ((), ())), preferred_element_type=f32
            )
            weights[d, k, :, 128:256] = turned.astype(bf16)
        return carry

    lax.fori_loop(0, MODES, one_mode, 0, unroll=2)


def send_kernel(along_rows, slots, coefs, *rest):
    lane = lane_numbers()
    bi, bj = device_block(lax.axis_index("chaos"))
    if along_rows:
        shift, stride, place = jnp.where(bi == 0, 0, 16), 16, lane >> 4
    else:
        shift, stride, place = jnp.where(bj == 0, 0, 114), 2, (lane & 15) >> 1
    sent = rest[-1]
    for r in range(8):
        total = jnp.zeros((8, 128), f32)
        for q in range(8):
            at, h = 4 * q + r // 2, r % 2
            block = slots[at, 8 * h : 8 * h + 8, :]
            total = jnp.where(place == q, pltpu.roll(block, lax.rem(shift + stride * q, 128), 1), total)
        sent[8 * r : 8 * r + 8, :] = total
    sent[64:80, :] = coefs[0:16, :]


def gather_blocks(spread, offsets, k, d):
    rows = []
    shift_one, shift_two = offsets[0, k], offsets[1, k]
    for at in (d + shift_one, d + shift_two, d + 8 - shift_one, d + 8 - shift_two):
        start = pl.multiple_of(512 * k + 64 * lax.rem(at, 8), 64)
        rows.append(spread[pl.ds(start, 64), :])
    return jnp.concatenate(rows, axis=0)


def again_kernel(columns_out, after, sent):
    sent[...] = columns_out[...]


def inner_kernel(slots, coefs, weights, offsets_at, after, also_after, out, faces, spread, offsets, arrived):
    copy = pltpu.make_async_copy(offsets_at, offsets, arrived.at[0])
    copy.start()
    inner_operator(slots, coefs, weights, offsets, copy, out, faces, spread)


def inner_operator(slots, coefs, weights, offsets, offsets_copy, out, faces, spread):
    lane = lane_numbers()
    column = lane & 15
    even = lane & 1 == 0
    bi, bj = device_block(lax.axis_index("chaos"))
    top, bottom = lane < 16, lane >= 112
    left, right = column < 2, column >= 14
    left_half = column < 8
    unit_first, unit_second, unit_third = unit_masks(lane)
    row_edge = ((bi == 0) & top) | ((bi == 3) & bottom)
    column_edge = ((bj == 0) & left) | ((bj == 7) & right)

    def neighbours(block, beside, sides):
        return (
            jnp.where(top, beside, roll(block, 16)),
            jnp.where(bottom, beside, roll(block, -16)),
            jnp.where(left, sides, roll(block, 2)),
            jnp.where(right, sides, roll(block, -2)),
            jnp.where(even, roll(block, -1), roll(block, 1)),
        )

    for h in range(2):
        center = coefs[8 * h : 8 * h + 8, :]
        beside = coefs[16 + 8 * h : 24 + 8 * h, :]
        sides = coefs[32 + 8 * h : 40 + 8 * h, :]
        for face, other in enumerate(neighbours(center, beside, sides)):
            weight = (center + other) * 0.5
            for k in range(8 * h, min(8 * h + 8, MODES + 1)):
                faces[5 * k + face] = jnp.broadcast_to(weight[k - 8 * h : k - 8 * h + 1], (8, 128))

    def one_slot(s, carry):
        units = slots[s, 16:24, :]
        opened = jnp.where(unit_third, units, roll(units, 32))
        opened = jnp.where(unit_second, opened, roll(opened, 16))
        opened = jnp.where(unit_first, opened, roll(opened, 8))
        halves = []
        for h in range(2):
            block = slots[s, 8 * h : 8 * h + 8, :]
            beside = jnp.where(row_edge, block, roll(units, -(80 + 32 * h)))
            sides = jnp.where(left_half, roll(opened, -(16 + 4 * h)), roll(opened, 12 - 4 * h))
            sides = jnp.where(column_edge, block, sides)
            others = neighbours(block, beside, sides)
            halves.append((block, [block - other for other in others]))

        def diffuse(k):
            sums = []
            for block, steps in halves:
                total = faces[5 * k] * steps[0]
                for face in range(1, 5):
                    total = total + faces[5 * k + face] * steps[face]
                sums.append(total)
            return sums

        for h, total in enumerate(diffuse(0)):
            out[s, 8 * h : 8 * h + 8, :] = halves[h][0] + total
        for k in range(MODES):
            total = jnp.concatenate(diffuse(k + 1), axis=0)
            high = total.astype(bf16)
            low = (total - high.astype(f32)).astype(bf16)
            at = pl.ds(pl.multiple_of(512 * k + 16 * s, 16), 16)
            spread[at, 0:128] = high
            spread[at, 128:256] = low
        return carry

    lax.fori_loop(0, 32, one_slot, 0, unroll=8)
    offsets_copy.wait()

    def one_block(d, carry):
        total = jnp.zeros((64, 256), f32)
        for k in range(MODES):
            blocks = gather_blocks(spread, offsets, k, d)
            total = total + jnp.dot(weights[d, k], blocks, preferred_element_type=f32)
        mixed = total[:, :128] + total[:, 128:]
        for part in range(4):
            out[4 * d + part] = out[4 * d + part] + mixed[16 * part : 16 * part + 16]
        return carry

    lax.fori_loop(0, 8, one_block, 0, unroll=8)


def wait_blocks(source, target, left):
    for d in range(8):
        part = slice(4 * d, 4 * d + 4)
        pltpu.make_async_copy(source.at[part], target.at[part], left.at[d]).wait()


def edge_kernel(rows_out, rows_in, columns_out, columns_first, columns_later, weights, offsets_at, inner, target, steps, spread, columns_in, out, left,
    offsets, arrived,
):
    bi, bj = device_block(lax.axis_index("chaos"))
    on_row = (bi == 0) | (bi == 3)
    on_column = (bj == 0) | (bj == 7)
    offsets_copy = pltpu.make_async_copy(offsets_at, offsets, arrived.at[0])
    offsets_copy.start()

    @pl.when(jnp.logical_not(on_row | on_column))
    def _():
        copy = pltpu.make_async_copy(inner, target, left.at[0])
        copy.start()
        copy.wait()
        offsets_copy.wait()

    early = lax.axis_index("sx") == 0

    @pl.when(on_column & early)
    def _():
        columns_in[...] = columns_first[...]

    @pl.when(jnp.logical_not(on_column & early))
    def _():
        columns_in[...] = columns_later[...]

    @pl.when(on_row | on_column)
    def _():
        edge_faces(
            bi, bj, on_row, on_column, rows_out, rows_in, columns_out, columns_in, weights, offsets, inner, out, steps, spread, target, left,
            offsets_copy,
        )
        wait_blocks(out, target, left)


def edge_faces(
    bi, bj, on_row, on_column, rows_out, rows_in, columns_out, columns_in, weights, offsets, inner, out, steps, spread,
    target, left, offsets_copy,
):
    lane = lane_numbers()
    column = lane & 15
    for r in range(8):
        rows = slice(8 * r, 8 * r + 8)
        step = rows_out[rows, :] - rows_in[rows, :]
        for bit in (1, 2, 4):
            outer, inner_bit = lane & (16 * bit) != 0, lane & (2 * bit) != 0
            step = jnp.where(
                outer == inner_bit, step, jnp.where(outer, roll(step, 14 * bit), roll(step, -14 * bit))
            )
        steps[rows, :] = step
        steps[64 + 8 * r : 72 + 8 * r, :] = columns_out[rows, :] - columns_in[rows, :]
    row_own, row_other = jnp.where(bi == 0, 0, 16), jnp.where(bi == 0, 16, 0)
    column_own, column_other = jnp.where(bj == 0, 0, 114), jnp.where(bj == 0, 114, 0)
    row_share = jnp.where(on_row, 0.5, 0.0)
    column_share = jnp.where(on_column, 0.5, 0.0)
    factors = []
    for h in range(2):
        terms = slice(64 + 8 * h, 72 + 8 * h)
        row = pltpu.roll(rows_out[terms, :], row_own, 1) + pltpu.roll(rows_in[terms, :], row_other, 1)
        row = jnp.where(lane < 8, row, roll(row, 56))
        row = jnp.where(lane & 63 < 4, row, roll(row, 28))
        row = jnp.where(lane & 31 < 2, row, roll(row, 14))
        side = pltpu.roll(columns_out[terms, :], column_own, 1) + pltpu.roll(
            columns_in[terms, :], column_other, 1
        )
        row, side = row * row_share, side * column_share
        joined = jnp.where(column < 2, side, roll(side, 2))
        joined = jnp.where(column < 4, joined, jnp.where(column < 6, roll(row, 4), roll(row, 6)))
        factors.append(jnp.where(column < 8, joined, 0.0))
    wide_factors = [
        jnp.broadcast_to(factors[k // 8][k % 8 : k % 8 + 1, :], (8, 128)) for k in range(MODES + 1)
    ]
    low_part = column & 2 != 0
    first_two, first_four, first_six = column < 2, column < 4, column < 6

    def scaled(k, step):
        return wide_factors[k] * step

    for q in range(8):
        for r in range(4):
            halves = []
            for half in range(2):
                at = 8 * (2 * r + half)
                row, side = steps[at : at + 8, :], steps[64 + at : 72 + at, :]
                step = jnp.where(first_two, roll(side, -2 * q), roll(side, 2 - 2 * q))
                other = jnp.where(first_six, roll(row, 4 - 2 * q), roll(row, 6 - 2 * q))
                halves.append(jnp.where(first_four, step, other))
            at = 64 * q + 16 * r
            for k in range(MODES):
                parts = []
                for step in halves:
                    total = scaled(k + 1, step)
                    high = total.astype(bf16).astype(f32)
                    parts.append(jnp.where(low_part, total - high, total))
                spread[512 * k + at : 512 * k + at + 16, :] = jnp.concatenate(parts, axis=0).astype(bf16)
            for half, step in enumerate(halves):
                start = 128 + at + 8 * half
                steps[start : start + 8, :] = jnp.where(low_part, 0.0, scaled(0, step))
    from_lane = lax.broadcasted_iota(jnp.int32, (128, 128), 0)
    to_lane = lax.broadcasted_iota(jnp.int32, (128, 128), 1)
    from_column, from_row, plane = from_lane & 15, from_lane >> 4, from_lane & 1
    side_to = 16 * from_row + jnp.where(bj == 0, 0, 14) + plane
    row_to = jnp.where(bi == 0, 0, 112) + 2 * from_row + plane
    lands = jnp.where(from_column < 4, side_to, row_to)
    place = jnp.where((from_column < 8) & (lands == to_lane), 1.0, 0.0).astype(bf16)
    place = jnp.concatenate([place] * 3, axis=0)
    offsets_copy.wait()

    def one_block(d, carry):
        total = steps[pl.ds(pl.multiple_of(128 + 64 * d, 64), 64), :]
        for k in range(MODES):
            blocks = gather_blocks(spread, offsets, k, d)
            total = total + jnp.dot(weights[d, k], blocks, preferred_element_type=f32)
        high = total.astype(bf16)
        rest = total - high.astype(f32)
        middle = rest.astype(bf16)
        low = (rest - middle.astype(f32)).astype(bf16)
        placed = jnp.dot(jnp.concatenate([high, middle, low], axis=1), place, preferred_element_type=f32)
        for part in range(4):
            out[4 * d + part] = inner[4 * d + part] + placed[16 * part : 16 * part + 16]
        pltpu.make_async_copy(out.at[pl.ds(4 * d, 4)], target.at[pl.ds(4 * d, 4)], left.at[d]).start()
        return carry

    lax.fori_loop(0, 8, one_block, 0, unroll=8)


def finish_kernel(field, slots, lower_bound, upper_bound, target, out, left):
    low = chunk_masks(lane_numbers())
    lower_end = jnp.full((8, 128), lower_bound[0], f32)
    upper_end = jnp.full((8, 128), upper_bound[0], f32)
    middle = (upper_end + lower_end) * 0.5
    half_width = (upper_end - lower_end) * 0.5
    spread_ratio = middle / half_width
    factor_now = 1.0 / spread_ratio
    factor_next = 1.0 / (2.0 * spread_ratio - factor_now)
    residual_scale = 2.0 * factor_next / half_width
    field_scale = (1.0 + factor_next * factor_now) / middle + residual_scale
    applied_scale = residual_scale / middle
    copies = []
    for bi in range(4):
        for h in range(2):
            terms = slice(8 * h, 8 * h + 8)
            rows = swap_chunks([slots[block_device(bi, bj), terms, :] for bj in range(8)], low)
            for i in range(8):
                at = 8 * bi + i
                out[terms, at, :] = field_scale * field[terms, at, :] - applied_scale * rows[i]
        part = pl.ds(8 * bi, 8)
        copies.append(pltpu.make_async_copy(out.at[:, part, :], target.at[:, part, :], left.at[bi]))
        copies[-1].start()
    for copy in copies:
        copy.wait()


def from_hbm(array):
    return pltpu.with_memory_space_constraint(array, pltpu.HBM)


def in_any():
    return pl.BlockSpec(memory_space=pl.ANY)


def in_hbm():
    return pl.BlockSpec(memory_space=pltpu.HBM)


def in_vmem():
    return pl.BlockSpec(memory_space=pltpu.VMEM)


def in_smem():
    return pl.BlockSpec(memory_space=pltpu.SMEM)


def call(kernel, ins, outs, scratch=(), cost=None, limit=32, aliases=None, name=None, out_specs=None):
    return pl.pallas_call(
        kernel,
        out_shape=outs,
        in_specs=ins,
        out_specs=out_specs or jax.tree.map(lambda _: in_vmem(), outs),
        scratch_shapes=scratch,
        cost_estimate=cost,
        input_output_aliases=aliases or {},
        compiler_params=pltpu.CompilerParams(vmem_limit_bytes=limit * 2**20),
        name=name or kernel.__name__,
    )


def per_device(right_side, mean_coef, mode_coef, coupling, offsets, lower_bound, upper_bound):
    shape = jax.ShapeDtypeStruct
    slots = call(
        pack_kernel,
        [in_hbm()],
        pltpu.HBM((32, 24, 128), f32),
        [
            pltpu.VMEM((16, 32, 128), f32),
            pltpu.VMEM((32, 24, 128), f32),
            pltpu.SemaphoreType.DMA((4,)),
            pltpu.SemaphoreType.DMA((32,)),
        ],
        out_specs=in_hbm(),
        limit=32,
    )(from_hbm(right_side))
    held = lax.all_to_all(slots, "chaos", 0, 0, tiled=True)
    offsets = offsets.T
    weights, coefs = call(
        prepare_kernel,
        [in_hbm(), in_smem(), in_hbm(), in_hbm()],
        (pltpu.VMEM((8, MODES, 64, 256), bf16), pltpu.VMEM((48, 128), f32)),
        [
            pltpu.VMEM((16 * MODES, 4096), bf16),
            pltpu.VMEM((512 * MODES, 128), f32),
            pltpu.VMEM((16, 32, 128), f32),
            pltpu.VMEM((8, 8, 128), f32),
            pltpu.SemaphoreType.DMA((3,)),
        ],
        pl.CostEstimate(flops=2**27, bytes_accessed=2**22, transcendentals=0),
        limit=32,
    )(from_hbm(coupling.reshape(16 * MODES, 4096)), offsets, from_hbm(mean_coef), from_hbm(mode_coef))
    def index(device, sx, sy):
        return (device * 4 + sx % 4) * 4 + sy % 4

    row_pairs, early_pairs, late_pairs = [], [], []
    for sx in range(4):
        for sy in range(4):
            for bj in range(8):
                low, high = block_device(0, bj), block_device(3, bj)
                row_pairs.append((index(high, sx, sy), index(low, sx + 1, sy)))
                row_pairs.append((index(low, sx, sy), index(high, sx - 1, sy)))
            for bi in range(4):
                low, high = block_device(bi, 0), block_device(bi, 7)
                pairs = early_pairs if sx == 0 else late_pairs
                pairs.append((index(high, sx, sy), index(low, sx, sy + 1)))
                pairs.append((index(low, sx, sy), index(high, sx, sy - 1)))
    axes = ("chaos", "sx", "sy")
    message = shape((80, 128), f32)
    offsets_scratch = [pltpu.SMEM((2, MODES), jnp.int32), pltpu.SemaphoreType.DMA((1,))]
    scratch = [
        pltpu.VMEM((5 * MODES + 5, 8, 128), f32),
        pltpu.VMEM((512 * MODES, 256), bf16),
    ] + offsets_scratch
    inner_cost = pl.CostEstimate(flops=2**32, bytes_accessed=2**24, transcendentals=0)
    inner_shape = pltpu.VMEM((32, 16, 128), f32)
    columns_out = call(
        functools.partial(send_kernel, False), [in_vmem()] * 2 + [in_any()], message, name="send_columns"
    )(held, coefs, coefs)
    columns_first = lax.ppermute(columns_out, axes, early_pairs)
    rows_out = call(
        functools.partial(send_kernel, True), [in_vmem()] * 2 + [in_any()], message, name="send_rows"
    )(held, coefs, columns_out)
    rows_in = lax.ppermute(rows_out, axes, row_pairs)
    columns_again = call(again_kernel, [in_vmem(), in_any()], message, name="send_again")(
        columns_out, rows_out
    )
    columns_later = lax.ppermute(columns_again, axes, late_pairs)
    inner = call(
        inner_kernel,
        [in_vmem()] * 3 + [in_any()] * 3,
        inner_shape,
        scratch,
        inner_cost,
    )(held, coefs, weights, offsets, columns_again, columns_first)
    applied = call(
        edge_kernel,
        [in_vmem()] * 6 + [in_any(), in_vmem()],
        pltpu.HBM((32, 16, 128), f32),
        [
            pltpu.VMEM((128 + 512, 128), f32),
            pltpu.VMEM((512 * MODES, 128), bf16),
            pltpu.VMEM((80, 128), f32),
            pltpu.VMEM((32, 16, 128), f32),
            pltpu.SemaphoreType.DMA((8,)),
        ]
        + offsets_scratch,
        out_specs=in_hbm(),
    )(rows_out, rows_in, columns_out, columns_first, columns_later, weights, offsets, inner)
    returned = lax.all_to_all(applied, "chaos", 0, 0, tiled=True)
    return call(
        finish_kernel,
        [in_vmem()] * 2 + [in_smem()] * 2,
        pltpu.HBM(right_side.shape, f32),
        [pltpu.VMEM(right_side.shape, f32), pltpu.SemaphoreType.DMA((4,))],
        out_specs=in_hbm(),
    )(right_side, returned, lower_bound, upper_bound)


def solution(mesh):
    return jax.shard_map(
        per_device,
        mesh=mesh,
        in_specs=(P("chaos", "sx", "sy"), P("sx", "sy"), P(None, "sx", "sy"), P(), P(), P(), P()),
        out_specs=P("chaos", "sx", "sy"),
        check_vma=False,
    )
```

```python
import functools

import jax
import jax.numpy as jnp
from jax import lax
from jax.experimental import pallas as pl
from jax.experimental.pallas import tpu as pltpu
from jax.sharding import PartitionSpec as P

f32 = jnp.float32
bf16 = jnp.bfloat16
MODES = 10
OUTER = ((2, 2), (3, 2), (3, 1), (2, 0), (2, 3), (1, 1), (1, 2), (2, 1))
INNER = ((0, 2), (0, 1), (0, 0), (1, 0), (3, 0), (3, 3), (0, 3), (1, 3))


def block_device(bi, bj):
    x, y = (OUTER if bi in (0, 3) else INNER)[bj]
    return y * 8 + x * 2 + (0, 0, 1, 1)[bi]


def device_block(index):
    core, chip = index % 2, index // 2
    halves = []
    for half in range(2):
        bits = 0
        for outer, chips in ((1, OUTER), (0, INNER)):
            for bj, (x, y) in enumerate(chips):
                if (4 * y + x) // 8 == half:
                    bits |= (8 * outer + bj) << (4 * ((4 * y + x) % 8))
        halves.append(bits - 2**32 if bits >= 2**31 else bits)
    entry = (jnp.where(chip < 8, halves[0], halves[1]) >> (4 * (chip % 8))) & 15
    bi = jnp.where(entry >= 8, 3 * core, 1 + core)
    return bi, entry % 8


FIRST = block_device(0, 0)


def lane_numbers():
    return lax.broadcasted_iota(jnp.int32, (8, 128), 1)


def roll(value, shift):
    if isinstance(shift, int):
        shift = shift % 128
        if shift == 0:
            return value
    return pltpu.roll(value, shift, 1)


def chunk_masks(lane):
    return {step: lane & (16 * step) == 0 for step in (1, 2, 4)}


def swap_chunks(rows, low):
    rows = list(rows)
    for step in (1, 2, 4):
        for i in range(8):
            if i & step == 0:
                a, b = rows[i], rows[i + step]
                rows[i] = jnp.where(low[step], a, roll(b, 16 * step))
                rows[i + step] = jnp.where(low[step], roll(a, -16 * step), b)
    return rows


def unit_masks(lane):
    return lane & 31 < 8, lane & 63 < 16, lane < 32


def pack_kernel(source, target, field, slots, arrived, left):
    copies = [
        pltpu.make_async_copy(
            source.at[:, 8 * bi : 8 * bi + 8, :], field.at[:, 8 * bi : 8 * bi + 8, :], arrived.at[bi]
        )
        for bi in range(4)
    ]
    for copy in copies:
        copy.start()
    lane = lane_numbers()
    low = chunk_masks(lane)
    unit_first, unit_second, unit_third = unit_masks(lane)
    column = lane & 15
    upper, unit_half = column >= 8, column < 4
    first_half = lane < 64
    for copy in copies:
        copy.wait()
    leaving = []
    for bi in range(4):
        blocks, above, below = [], [], []
        for h in range(2):
            terms = slice(8 * h, 8 * h + 8)
            rows = [field[terms, 8 * bi + i, :] for i in range(8)]
            blocks.append(swap_chunks(rows, low))
            above.append(field[terms, 8 * bi - 1, :] if bi > 0 else rows[0])
            below.append(field[terms, 8 * bi + 8, :] if bi < 3 else rows[7])
        beside = [below[0], above[0], below[1], above[1]]
        for step in (1, 2):
            for i in range(4):
                if i & step == 0:
                    a, b = beside[i], beside[i + step]
                    beside[i] = jnp.where(low[step], a, roll(b, 16 * step))
                    beside[i + step] = jnp.where(low[step], roll(a, -16 * step), b)
        beside = [roll(row, 64) for row in beside] + beside
        for bj in range(8):
            at = block_device(bi, bj)
            units = []
            for h in range(2):
                slots[at, 8 * h : 8 * h + 8, :] = blocks[h][bj]
                side = jnp.where(upper, blocks[h][(bj - 1) % 8], blocks[h][(bj + 1) % 8])
                units.append(roll(side, 2 + 4 * h))
            row = jnp.where(unit_half, units[0], units[1])
            row = jnp.where(unit_first, row, roll(row, -8))
            row = jnp.where(unit_second, row, roll(row, -16))
            row = jnp.where(unit_third, row, roll(row, -32))
            slots[at, 16:24, :] = jnp.where(first_half, row, beside[bj])
        for bj in range(8):
            at = block_device(bi, bj)
            leaving.append(pltpu.make_async_copy(slots.at[at], target.at[at], left.at[at]))
            leaving[-1].start()
    for copy in leaving:
        copy.wait()


def prepare_kernel(
    coupling_at, offsets_at, mean_at, mode_at, lower_bound, upper_bound, weights, coefs, scales, coupling, pairs, tile,
    parts, offsets, arrived,
):
    copies = [
        pltpu.make_async_copy(mean_at, tile.at[0], arrived.at[0]),
        pltpu.make_async_copy(mode_at, tile.at[1 : MODES + 1], arrived.at[1]),
        pltpu.make_async_copy(coupling_at, coupling, arrived.at[2]),
        pltpu.make_async_copy(offsets_at, offsets, arrived.at[3]),
    ]
    for copy in copies:
        copy.start()
    tile[MODES + 1 :] = jnp.zeros((15 - MODES, 32, 128), f32)
    lane = lane_numbers()
    low = chunk_masks(lane)
    first = lane < 64
    left_half = lane & 15 < 8
    bi, bj = device_block(lax.axis_index("chaos"))
    copies[0].wait()
    copies[1].wait()
    for h in range(2):
        terms = slice(8 * h, 8 * h + 8)
        blocks = swap_chunks([tile[terms, 8 * bi + i, :] for i in range(8)], low)
        for j in range(8):
            parts[j] = blocks[j]
        coefs[8 * h : 8 * h + 8, :] = parts[bj]
        above = tile[terms, lax.rem(8 * bi + 31, 32), :]
        below = tile[terms, lax.rem(8 * bi + 8, 32), :]
        coefs[16 + 8 * h : 24 + 8 * h, :] = jnp.where(
            first,
            pltpu.roll(above, lax.rem(128 - 16 * bj, 128), 1),
            pltpu.roll(below, lax.rem(240 - 16 * bj, 128), 1),
        )
        coefs[32 + 8 * h : 40 + 8 * h, :] = jnp.where(
            left_half, roll(parts[lax.rem(bj + 7, 8)], -14), roll(parts[lax.rem(bj + 1, 8)], 14)
        )
    out_row = lax.broadcasted_iota(jnp.int32, (64, 128), 0)
    out_col = lax.broadcasted_iota(jnp.int32, (64, 128), 1)
    pick = jnp.where(out_col & 63 == out_row, 1.0, 0.0).astype(bf16)
    wide = out_col < 64
    lower_end = jnp.full((8, 128), lower_bound[0], f32)
    upper_end = jnp.full((8, 128), upper_bound[0], f32)
    middle = (upper_end + lower_end) * 0.5
    half_width = (upper_end - lower_end) * 0.5
    spread_ratio = middle / half_width
    factor_now = 1.0 / spread_ratio
    factor_next = 1.0 / (2.0 * spread_ratio - factor_now)
    residual_scale = 2.0 * factor_next / half_width
    field_scale = (1.0 + factor_next * factor_now) / middle + residual_scale
    applied_scale = residual_scale / middle
    scales[0:8, :] = field_scale
    scales[8:16, :] = applied_scale
    copies[3].wait()
    copies[2].wait()

    def one_mode(k, carry):
        base = pl.multiple_of(512 * k, 512)
        for m in range(32):
            both = coupling[pl.ds(pl.multiple_of(16 * k, 16), 16), 128 * m : 128 * m + 128].astype(f32)
            one, two = both[:8], both[8:]
            pairs[pl.ds(base + 2 * m, 8, 64), :] = jnp.where(first, one, roll(two, 64))
            pairs[pl.ds(base + 2 * m + 1, 8, 64), :] = jnp.where(first, roll(one, 64), two)
        shift_one, shift_two = offsets[0, k], offsets[1, k]
        for d in range(8):
            weights[d, k, :, 0:128] = pairs[pl.ds(base + 64 * d, 64), :].astype(bf16)
            from_one = lax.rem(d + 8 - shift_one, 8)
            from_two = lax.rem(d + 8 - shift_two, 8)
            one = pairs[pl.ds(pl.multiple_of(base + 64 * from_one, 64), 64), :]
            two = pairs[pl.ds(pl.multiple_of(base + 64 * from_two, 64), 64), :]
            stack = jnp.concatenate([jnp.where(wide, one, 0.0), jnp.where(wide, 0.0, two)], axis=0)
            turned = lax.dot_general(
                pick, stack.astype(bf16), (((1,), (1,)), ((), ())), preferred_element_type=f32
            )
            weights[d, k, :, 128:256] = turned.astype(bf16)
        return carry

    lax.fori_loop(0, MODES, one_mode, 0, unroll=5)


def send_kernel(along_rows, slots, coefs, *rest):
    lane = lane_numbers()
    bi, bj = device_block(lax.axis_index("chaos"))
    if along_rows:
        shift, stride, place = jnp.where(bi == 0, 0, 16), 16, lane >> 4
    else:
        shift, stride, place = jnp.where(bj == 0, 0, 114), 2, (lane & 15) >> 1
    sent = rest[-1]
    for r in range(8):
        total = jnp.zeros((8, 128), f32)
        for q in range(8):
            at, h = 4 * q + r // 2, r % 2
            block = slots[at, 8 * h : 8 * h + 8, :]
            total = jnp.where(place == q, pltpu.roll(block, lax.rem(shift + stride * q, 128), 1), total)
        sent[8 * r : 8 * r + 8, :] = total
    sent[64:80, :] = coefs[0:16, :]


def gather_blocks(spread, offsets, k, d):
    rows = []
    shift_one, shift_two = offsets[0, k], offsets[1, k]
    for at in (d + shift_one, d + shift_two, d + 8 - shift_one, d + 8 - shift_two):
        start = pl.multiple_of(512 * k + 64 * lax.rem(at, 8), 64)
        rows.append(spread[pl.ds(start, 64), :])
    return jnp.concatenate(rows, axis=0)


def again_kernel(columns_out, after, sent):
    sent[...] = columns_out[...]


def inner_kernel(first, slots, coefs, weights, offsets_at, *rest):
    out, faces, spread, offsets, arrived = rest[-5:]
    bi, bj = device_block(lax.axis_index("chaos"))
    before = (lax.axis_index("sx") == 0) & (bi == 0) & (bj > 0) & (bj < 7)

    @pl.when(before == first)
    def _():
        copy = pltpu.make_async_copy(offsets_at, offsets, arrived.at[0])
        copy.start()
        inner_operator(slots, coefs, weights, offsets, copy, out, faces, spread)


def inner_operator(slots, coefs, weights, offsets, offsets_copy, out, faces, spread):
    lane = lane_numbers()
    column = lane & 15
    even = lane & 1 == 0
    bi, bj = device_block(lax.axis_index("chaos"))
    top, bottom = lane < 16, lane >= 112
    left, right = column < 2, column >= 14
    left_half = column < 8
    unit_first, unit_second, unit_third = unit_masks(lane)
    row_edge = ((bi == 0) & top) | ((bi == 3) & bottom)
    column_edge = ((bj == 0) & left) | ((bj == 7) & right)

    def neighbours(block, beside, sides):
        return (
            jnp.where(top, beside, roll(block, 16)),
            jnp.where(bottom, beside, roll(block, -16)),
            jnp.where(left, sides, roll(block, 2)),
            jnp.where(right, sides, roll(block, -2)),
            jnp.where(even, roll(block, -1), roll(block, 1)),
        )

    for h in range(2):
        center = coefs[8 * h : 8 * h + 8, :]
        beside = coefs[16 + 8 * h : 24 + 8 * h, :]
        sides = coefs[32 + 8 * h : 40 + 8 * h, :]
        for face, other in enumerate(neighbours(center, beside, sides)):
            weight = (center + other) * 0.5
            for k in range(8 * h, min(8 * h + 8, MODES + 1)):
                faces[5 * k + face] = jnp.broadcast_to(weight[k - 8 * h : k - 8 * h + 1], (8, 128))

    def one_slot(s, carry):
        units = slots[s, 16:24, :]
        opened = jnp.where(unit_third, units, roll(units, 32))
        opened = jnp.where(unit_second, opened, roll(opened, 16))
        opened = jnp.where(unit_first, opened, roll(opened, 8))
        halves = []
        for h in range(2):
            block = slots[s, 8 * h : 8 * h + 8, :]
            beside = jnp.where(row_edge, block, roll(units, -(80 + 32 * h)))
            sides = jnp.where(left_half, roll(opened, -(16 + 4 * h)), roll(opened, 12 - 4 * h))
            sides = jnp.where(column_edge, block, sides)
            others = neighbours(block, beside, sides)
            halves.append((block, [block - other for other in others]))

        def diffuse(k):
            sums = []
            for block, steps in halves:
                total = faces[5 * k] * steps[0]
                for face in range(1, 5):
                    total = total + faces[5 * k + face] * steps[face]
                sums.append(total)
            return sums

        for h, total in enumerate(diffuse(0)):
            out[s, 8 * h : 8 * h + 8, :] = halves[h][0] + total
        for k in range(MODES):
            total = jnp.concatenate(diffuse(k + 1), axis=0)
            high = total.astype(bf16)
            low = (total - high.astype(f32)).astype(bf16)
            at = pl.ds(pl.multiple_of(512 * k + 16 * s, 16), 16)
            spread[at, 0:128] = high
            spread[at, 128:256] = low
        return carry

    lax.fori_loop(0, 32, one_slot, 0, unroll=8)
    offsets_copy.wait()

    def one_block(d, carry):
        total = jnp.zeros((64, 256), f32)
        for k in range(MODES):
            blocks = gather_blocks(spread, offsets, k, d)
            total = total + jnp.dot(weights[d, k], blocks, preferred_element_type=f32)
        mixed = total[:, :128] + total[:, 128:]
        for part in range(4):
            out[4 * d + part] = out[4 * d + part] + mixed[16 * part : 16 * part + 16]
        return carry

    lax.fori_loop(0, 8, one_block, 0, unroll=8)


def edge_kernel(rows_out, rows_in, columns_out, columns_first, columns_later, weights, offsets_at, inner, source, out, field, steps, spread, columns_in,
    offsets, arrived,
):
    bi, bj = device_block(lax.axis_index("chaos"))
    on_row = (bi == 0) | (bi == 3)
    on_column = (bj == 0) | (bj == 7)
    offsets_copy = pltpu.make_async_copy(offsets_at, offsets, arrived.at[0])
    offsets_copy.start()
    field_copy = pltpu.make_async_copy(source, field, arrived.at[1])
    field_copy.start()

    @pl.when(jnp.logical_not(on_row | on_column))
    def _():
        out[: 32 - FIRST] = inner[FIRST:]
        out[32 - FIRST :] = inner[:FIRST]
        offsets_copy.wait()

    early = lax.axis_index("sx") == 0

    @pl.when(on_column & early)
    def _():
        columns_in[...] = columns_first[...]

    @pl.when(jnp.logical_not(on_column & early))
    def _():
        columns_in[...] = columns_later[...]

    @pl.when(on_row | on_column)
    def _():
        edge_faces(
            bi, bj, on_row, on_column, rows_out, rows_in, columns_out, columns_in, weights, offsets, inner, out, steps, spread,
            offsets_copy,
        )

    field_copy.wait()


def edge_faces(
    bi, bj, on_row, on_column, rows_out, rows_in, columns_out, columns_in, weights, offsets, inner, out, steps, spread,
    offsets_copy,
):
    lane = lane_numbers()
    column = lane & 15
    for r in range(8):
        rows = slice(8 * r, 8 * r + 8)
        step = rows_out[rows, :] - rows_in[rows, :]
        for bit in (1, 2, 4):
            outer, inner_bit = lane & (16 * bit) != 0, lane & (2 * bit) != 0
            step = jnp.where(
                outer == inner_bit, step, jnp.where(outer, roll(step, 14 * bit), roll(step, -14 * bit))
            )
        steps[rows, :] = step
        steps[64 + 8 * r : 72 + 8 * r, :] = columns_out[rows, :] - columns_in[rows, :]
    row_own, row_other = jnp.where(bi == 0, 0, 16), jnp.where(bi == 0, 16, 0)
    column_own, column_other = jnp.where(bj == 0, 0, 114), jnp.where(bj == 0, 114, 0)
    row_share = jnp.where(on_row, 0.5, 0.0)
    column_share = jnp.where(on_column, 0.5, 0.0)
    factors = []
    for h in range(2):
        terms = slice(64 + 8 * h, 72 + 8 * h)
        row = pltpu.roll(rows_out[terms, :], row_own, 1) + pltpu.roll(rows_in[terms, :], row_other, 1)
        row = jnp.where(lane < 8, row, roll(row, 56))
        row = jnp.where(lane & 63 < 4, row, roll(row, 28))
        row = jnp.where(lane & 31 < 2, row, roll(row, 14))
        side = pltpu.roll(columns_out[terms, :], column_own, 1) + pltpu.roll(
            columns_in[terms, :], column_other, 1
        )
        row, side = row * row_share, side * column_share
        joined = jnp.where(column < 2, side, roll(side, 2))
        joined = jnp.where(column < 4, joined, jnp.where(column < 6, roll(row, 4), roll(row, 6)))
        factors.append(jnp.where(column < 8, joined, 0.0))
    wide_factors = [
        jnp.broadcast_to(factors[k // 8][k % 8 : k % 8 + 1, :], (8, 128)) for k in range(MODES + 1)
    ]
    low_part = column & 2 != 0
    first_two, first_four, first_six = column < 2, column < 4, column < 6

    def scaled(k, step):
        return wide_factors[k] * step

    for q in range(8):
        for r in range(4):
            halves = []
            for half in range(2):
                at = 8 * (2 * r + half)
                row, side = steps[at : at + 8, :], steps[64 + at : 72 + at, :]
                step = jnp.where(first_two, roll(side, -2 * q), roll(side, 2 - 2 * q))
                other = jnp.where(first_six, roll(row, 4 - 2 * q), roll(row, 6 - 2 * q))
                halves.append(jnp.where(first_four, step, other))
            at = 64 * q + 16 * r
            for k in range(MODES):
                parts = []
                for step in halves:
                    total = scaled(k + 1, step)
                    high = total.astype(bf16).astype(f32)
                    parts.append(jnp.where(low_part, total - high, total))
                spread[512 * k + at : 512 * k + at + 16, :] = jnp.concatenate(parts, axis=0).astype(bf16)
            for half, step in enumerate(halves):
                start = 128 + at + 8 * half
                steps[start : start + 8, :] = jnp.where(low_part, 0.0, scaled(0, step))
    from_lane = lax.broadcasted_iota(jnp.int32, (128, 128), 0)
    to_lane = lax.broadcasted_iota(jnp.int32, (128, 128), 1)
    from_column, from_row, plane = from_lane & 15, from_lane >> 4, from_lane & 1
    side_to = 16 * from_row + jnp.where(bj == 0, 0, 14) + plane
    row_to = jnp.where(bi == 0, 0, 112) + 2 * from_row + plane
    lands = jnp.where(from_column < 4, side_to, row_to)
    place = jnp.where((from_column < 8) & (lands == to_lane), 1.0, 0.0).astype(bf16)
    place = jnp.concatenate([place] * 3, axis=0)
    offsets_copy.wait()

    def one_block(d, carry):
        total = steps[pl.ds(pl.multiple_of(128 + 64 * d, 64), 64), :]
        for k in range(MODES):
            blocks = gather_blocks(spread, offsets, k, d)
            total = total + jnp.dot(weights[d, k], blocks, preferred_element_type=f32)
        high = total.astype(bf16)
        rest = total - high.astype(f32)
        middle = rest.astype(bf16)
        low = (rest - middle.astype(f32)).astype(bf16)
        placed = jnp.dot(jnp.concatenate([high, middle, low], axis=1), place, preferred_element_type=f32)
        to = lax.rem(4 * d + 32 - FIRST, 32)
        for part in range(4):
            out[to + part] = inner[4 * d + part] + placed[16 * part : 16 * part + 16]
        return carry

    lax.fori_loop(0, 8, one_block, 0, unroll=8)


def finish_kernel(field, slots, scales, target, out, left):
    low = chunk_masks(lane_numbers())
    field_scale, applied_scale = scales[0:8, :], scales[8:16, :]
    copies = []
    for bi in range(4):
        for h in range(2):
            terms = slice(8 * h, 8 * h + 8)
            rows = swap_chunks([slots[(block_device(bi, bj) - FIRST) % 32, terms, :] for bj in range(8)], low)
            for i in range(8):
                at = 8 * bi + i
                out[terms, at, :] = field_scale * field[terms, at, :] - applied_scale * rows[i]
        part = pl.ds(8 * bi, 8)
        copies.append(pltpu.make_async_copy(out.at[:, part, :], target.at[:, part, :], left.at[bi]))
        copies[-1].start()
    for copy in copies:
        copy.wait()


def from_hbm(array):
    return pltpu.with_memory_space_constraint(array, pltpu.HBM)


def in_any():
    return pl.BlockSpec(memory_space=pl.ANY)


def in_hbm():
    return pl.BlockSpec(memory_space=pltpu.HBM)


def in_vmem():
    return pl.BlockSpec(memory_space=pltpu.VMEM)


def in_smem():
    return pl.BlockSpec(memory_space=pltpu.SMEM)


def call(kernel, ins, outs, scratch=(), cost=None, limit=32, aliases=None, name=None, out_specs=None):
    return pl.pallas_call(
        kernel,
        out_shape=outs,
        in_specs=ins,
        out_specs=out_specs or jax.tree.map(lambda _: in_vmem(), outs),
        scratch_shapes=scratch,
        cost_estimate=cost,
        input_output_aliases=aliases or {},
        compiler_params=pltpu.CompilerParams(vmem_limit_bytes=limit * 2**20),
        name=name or kernel.__name__,
    )


def per_device(right_side, mean_coef, mode_coef, coupling, offsets, lower_bound, upper_bound):
    shape = jax.ShapeDtypeStruct
    slots = call(
        pack_kernel,
        [in_hbm()],
        pltpu.HBM((32, 24, 128), f32),
        [
            pltpu.VMEM((16, 32, 128), f32),
            pltpu.VMEM((32, 24, 128), f32),
            pltpu.SemaphoreType.DMA((4,)),
            pltpu.SemaphoreType.DMA((32,)),
        ],
        out_specs=in_hbm(),
        limit=32,
    )(from_hbm(right_side))
    held = lax.all_to_all(slots, "chaos", 0, 0, tiled=True)
    offsets = from_hbm(offsets.T)
    weights, coefs, scales = call(
        prepare_kernel,
        [in_hbm()] * 4 + [in_smem()] * 2,
        (pltpu.VMEM((8, MODES, 64, 256), bf16), pltpu.VMEM((48, 128), f32), pltpu.VMEM((16, 128), f32)),
        [
            pltpu.VMEM((16 * MODES, 4096), bf16),
            pltpu.VMEM((512 * MODES, 128), f32),
            pltpu.VMEM((16, 32, 128), f32),
            pltpu.VMEM((8, 8, 128), f32),
            pltpu.SMEM((2, MODES), jnp.int32),
            pltpu.SemaphoreType.DMA((4,)),
        ],
        pl.CostEstimate(flops=2**27, bytes_accessed=2**22, transcendentals=0),
        limit=32,
    )(from_hbm(coupling.reshape(16 * MODES, 4096)), offsets, from_hbm(mean_coef), from_hbm(mode_coef), lower_bound, upper_bound)
    def index(device, sx, sy):
        return (device * 4 + sx % 4) * 4 + sy % 4

    row_pairs, early_pairs, late_pairs = [], [], []
    for sx in range(4):
        for sy in range(4):
            for bj in range(8):
                low, high = block_device(0, bj), block_device(3, bj)
                row_pairs.append((index(high, sx, sy), index(low, sx + 1, sy)))
                row_pairs.append((index(low, sx, sy), index(high, sx - 1, sy)))
            for bi in range(4):
                low, high = block_device(bi, 0), block_device(bi, 7)
                pairs = early_pairs if sx == 0 else late_pairs
                pairs.append((index(high, sx, sy), index(low, sx, sy + 1)))
                pairs.append((index(low, sx, sy), index(high, sx, sy - 1)))
    axes = ("chaos", "sx", "sy")
    message = shape((80, 128), f32)
    offsets_scratch = [pltpu.SMEM((2, MODES), jnp.int32), pltpu.SemaphoreType.DMA((1,))]
    scratch = [
        pltpu.VMEM((5 * MODES + 5, 8, 128), f32),
        pltpu.VMEM((512 * MODES, 256), bf16),
    ] + offsets_scratch
    inner_cost = pl.CostEstimate(flops=2**32, bytes_accessed=2**24, transcendentals=0)
    inner_shape = pltpu.VMEM((32, 16, 128), f32)
    columns_out = call(
        functools.partial(send_kernel, False), [in_vmem()] * 2 + [in_any()], message, name="send_columns"
    )(held, coefs, coefs)
    columns_first = lax.ppermute(columns_out, axes, early_pairs)
    inner = call(
        functools.partial(inner_kernel, True),
        [in_vmem()] * 3 + [in_hbm()] + [in_any()],
        inner_shape,
        scratch,
        inner_cost,
        name="inner_before",
    )(held, coefs, weights, offsets, columns_out)
    rows_out = call(
        functools.partial(send_kernel, True), [in_vmem()] * 2 + [in_any()], message, name="send_rows"
    )(held, coefs, inner)
    rows_in = lax.ppermute(rows_out, axes, row_pairs)
    columns_again = call(again_kernel, [in_vmem(), in_any()], message, name="send_again")(
        columns_out, rows_out
    )
    columns_later = lax.ppermute(columns_again, axes, late_pairs)
    inner = call(
        functools.partial(inner_kernel, False),
        [in_vmem()] * 3 + [in_hbm(), in_vmem()] + [in_any()] * 2,
        inner_shape,
        scratch,
        inner_cost,
        aliases={4: 0},
        name="inner_after",
    )(held, coefs, weights, offsets, inner, columns_again, columns_first)
    applied, field = call(
        edge_kernel,
        [in_vmem()] * 6 + [in_hbm(), in_vmem(), in_hbm()],
        (pltpu.VMEM((32, 16, 128), f32), pltpu.VMEM(right_side.shape, f32)),
        [
            pltpu.VMEM((128 + 512, 128), f32),
            pltpu.VMEM((512 * MODES, 128), bf16),
            pltpu.VMEM((80, 128), f32),
            pltpu.SMEM((2, MODES), jnp.int32),
            pltpu.SemaphoreType.DMA((2,)),
        ],
    )(
        rows_out, rows_in, columns_out, columns_first, columns_later, weights, offsets, inner, from_hbm(right_side)
    )
    turned = [[(FIRST + i) % 32 for i in range(32)]]
    returned = lax.all_to_all(applied, "chaos", 0, 0, tiled=True, axis_index_groups=turned)
    return call(
        finish_kernel,
        [in_vmem()] * 3,
        pltpu.HBM(right_side.shape, f32),
        [pltpu.VMEM(right_side.shape, f32), pltpu.SemaphoreType.DMA((4,))],
        out_specs=in_hbm(),
    )(field, returned, scales)


def solution(mesh):
    return jax.shard_map(
        per_device,
        mesh=mesh,
        in_specs=(P("chaos", "sx", "sy"), P("sx", "sy"), P(None, "sx", "sy"), P(), P(), P(), P()),
        out_specs=P("chaos", "sx", "sy"),
        check_vma=False,
    )
```

```python
import functools

import jax
import jax.numpy as jnp
from jax import lax
from jax.experimental import pallas as pl
from jax.experimental.pallas import tpu as pltpu
from jax.sharding import PartitionSpec as P

f32 = jnp.float32
bf16 = jnp.bfloat16
MODES = 10
OUTER = ((2, 2), (3, 2), (3, 1), (2, 0), (2, 3), (1, 1), (1, 2), (2, 1))
INNER = ((0, 2), (0, 1), (0, 0), (1, 0), (3, 0), (3, 3), (0, 3), (1, 3))


def block_device(bi, bj):
    x, y = (OUTER if bi in (0, 3) else INNER)[bj]
    return y * 8 + x * 2 + (0, 0, 1, 1)[bi]


def device_block(index):
    core, chip = index % 2, index // 2
    halves = []
    for half in range(2):
        bits = 0
        for outer, chips in ((1, OUTER), (0, INNER)):
            for bj, (x, y) in enumerate(chips):
                if (4 * y + x) // 8 == half:
                    bits |= (8 * outer + bj) << (4 * ((4 * y + x) % 8))
        halves.append(bits - 2**32 if bits >= 2**31 else bits)
    entry = (jnp.where(chip < 8, halves[0], halves[1]) >> (4 * (chip % 8))) & 15
    bi = jnp.where(entry >= 8, 3 * core, 1 + core)
    return bi, entry % 8


FIRST = block_device(0, 0)


def lane_numbers():
    return lax.broadcasted_iota(jnp.int32, (8, 128), 1)


def roll(value, shift):
    if isinstance(shift, int):
        shift = shift % 128
        if shift == 0:
            return value
    return pltpu.roll(value, shift, 1)


def chunk_masks(lane):
    return {step: lane & (16 * step) == 0 for step in (1, 2, 4)}


def swap_chunks(rows, low):
    rows = list(rows)
    for step in (1, 2, 4):
        for i in range(8):
            if i & step == 0:
                a, b = rows[i], rows[i + step]
                rows[i] = jnp.where(low[step], a, roll(b, 16 * step))
                rows[i + step] = jnp.where(low[step], roll(a, -16 * step), b)
    return rows


def unit_masks(lane):
    return lane & 31 < 8, lane & 63 < 16, lane < 32


def pack_kernel(source, target, field, slots, arrived, left):
    copies = [
        pltpu.make_async_copy(
            source.at[:, 8 * bi : 8 * bi + 8, :], field.at[:, 8 * bi : 8 * bi + 8, :], arrived.at[bi]
        )
        for bi in range(4)
    ]
    for copy in copies:
        copy.start()
    lane = lane_numbers()
    low = chunk_masks(lane)
    unit_first, unit_second, unit_third = unit_masks(lane)
    column = lane & 15
    upper, unit_half = column >= 8, column < 4
    first_half = lane < 64
    for copy in copies:
        copy.wait()
    leaving = []
    for bi in range(4):
        blocks, above, below = [], [], []
        for h in range(2):
            terms = slice(8 * h, 8 * h + 8)
            rows = [field[terms, 8 * bi + i, :] for i in range(8)]
            blocks.append(swap_chunks(rows, low))
            above.append(field[terms, 8 * bi - 1, :] if bi > 0 else rows[0])
            below.append(field[terms, 8 * bi + 8, :] if bi < 3 else rows[7])
        beside = [below[0], above[0], below[1], above[1]]
        for step in (1, 2):
            for i in range(4):
                if i & step == 0:
                    a, b = beside[i], beside[i + step]
                    beside[i] = jnp.where(low[step], a, roll(b, 16 * step))
                    beside[i + step] = jnp.where(low[step], roll(a, -16 * step), b)
        beside = [roll(row, 64) for row in beside] + beside
        for bj in range(8):
            at = block_device(bi, bj)
            units = []
            for h in range(2):
                slots[at, 8 * h : 8 * h + 8, :] = blocks[h][bj]
                side = jnp.where(upper, blocks[h][(bj - 1) % 8], blocks[h][(bj + 1) % 8])
                units.append(roll(side, 2 + 4 * h))
            row = jnp.where(unit_half, units[0], units[1])
            row = jnp.where(unit_first, row, roll(row, -8))
            row = jnp.where(unit_second, row, roll(row, -16))
            row = jnp.where(unit_third, row, roll(row, -32))
            slots[at, 16:24, :] = jnp.where(first_half, row, beside[bj])
        for bj in range(8):
            at = block_device(bi, bj)
            leaving.append(pltpu.make_async_copy(slots.at[at], target.at[at], left.at[at]))
            leaving[-1].start()
    for copy in leaving:
        copy.wait()


def prepare_kernel(
    coupling_at, offsets_at, mean_at, mode_at, lower_bound, upper_bound, weights, coefs, scales, coupling, pairs, tile,
    parts, offsets, arrived,
):
    copies = [
        pltpu.make_async_copy(mean_at, tile.at[0], arrived.at[0]),
        pltpu.make_async_copy(mode_at, tile.at[1 : MODES + 1], arrived.at[1]),
        pltpu.make_async_copy(coupling_at, coupling, arrived.at[2]),
        pltpu.make_async_copy(offsets_at, offsets, arrived.at[3]),
    ]
    for copy in copies:
        copy.start()
    tile[MODES + 1 :] = jnp.zeros((15 - MODES, 32, 128), f32)
    lane = lane_numbers()
    low = chunk_masks(lane)
    first = lane < 64
    left_half = lane & 15 < 8
    bi, bj = device_block(lax.axis_index("chaos"))
    copies[0].wait()
    copies[1].wait()
    for h in range(2):
        terms = slice(8 * h, 8 * h + 8)
        blocks = swap_chunks([tile[terms, 8 * bi + i, :] for i in range(8)], low)
        for j in range(8):
            parts[j] = blocks[j]
        coefs[8 * h : 8 * h + 8, :] = parts[bj]
        above = tile[terms, lax.rem(8 * bi + 31, 32), :]
        below = tile[terms, lax.rem(8 * bi + 8, 32), :]
        coefs[16 + 8 * h : 24 + 8 * h, :] = jnp.where(
            first,
            pltpu.roll(above, lax.rem(128 - 16 * bj, 128), 1),
            pltpu.roll(below, lax.rem(240 - 16 * bj, 128), 1),
        )
        coefs[32 + 8 * h : 40 + 8 * h, :] = jnp.where(
            left_half, roll(parts[lax.rem(bj + 7, 8)], -14), roll(parts[lax.rem(bj + 1, 8)], 14)
        )
    out_row = lax.broadcasted_iota(jnp.int32, (64, 128), 0)
    out_col = lax.broadcasted_iota(jnp.int32, (64, 128), 1)
    pick = jnp.where(out_col & 63 == out_row, 1.0, 0.0).astype(bf16)
    wide = out_col < 64
    lower_end = jnp.full((8, 128), lower_bound[0], f32)
    upper_end = jnp.full((8, 128), upper_bound[0], f32)
    middle = (upper_end + lower_end) * 0.5
    half_width = (upper_end - lower_end) * 0.5
    spread_ratio = middle / half_width
    factor_now = 1.0 / spread_ratio
    factor_next = 1.0 / (2.0 * spread_ratio - factor_now)
    residual_scale = 2.0 * factor_next / half_width
    field_scale = (1.0 + factor_next * factor_now) / middle + residual_scale
    applied_scale = residual_scale / middle
    scales[0:8, :] = field_scale
    scales[8:16, :] = applied_scale
    copies[3].wait()
    copies[2].wait()

    def one_mode(k, carry):
        base = pl.multiple_of(512 * k, 512)
        for m in range(32):
            both = coupling[pl.ds(pl.multiple_of(16 * k, 16), 16), 128 * m : 128 * m + 128].astype(f32)
            one, two = both[:8], both[8:]
            pairs[pl.ds(base + 2 * m, 8, 64), :] = jnp.where(first, one, roll(two, 64))
            pairs[pl.ds(base + 2 * m + 1, 8, 64), :] = jnp.where(first, roll(one, 64), two)
        shift_one, shift_two = offsets[0, k], offsets[1, k]
        for d in range(8):
            weights[d, k, :, 0:128] = pairs[pl.ds(base + 64 * d, 64), :].astype(bf16)
            from_one = lax.rem(d + 8 - shift_one, 8)
            from_two = lax.rem(d + 8 - shift_two, 8)
            one = pairs[pl.ds(pl.multiple_of(base + 64 * from_one, 64), 64), :]
            two = pairs[pl.ds(pl.multiple_of(base + 64 * from_two, 64), 64), :]
            stack = jnp.concatenate([jnp.where(wide, one, 0.0), jnp.where(wide, 0.0, two)], axis=0)
            turned = lax.dot_general(
                pick, stack.astype(bf16), (((1,), (1,)), ((), ())), preferred_element_type=f32
            )
            weights[d, k, :, 128:256] = turned.astype(bf16)
        return carry

    lax.fori_loop(0, MODES, one_mode, 0, unroll=5)


def send_kernel(along_rows, slots, coefs, *rest):
    lane = lane_numbers()
    bi, bj = device_block(lax.axis_index("chaos"))
    if along_rows:
        shift, stride, place = jnp.where(bi == 0, 0, 16), 16, lane >> 4
    else:
        shift, stride, place = jnp.where(bj == 0, 0, 114), 2, (lane & 15) >> 1
    sent = rest[-1]
    for r in range(8):
        total = jnp.zeros((8, 128), f32)
        for q in range(8):
            at, h = 4 * q + r // 2, r % 2
            block = slots[at, 8 * h : 8 * h + 8, :]
            total = jnp.where(place == q, pltpu.roll(block, lax.rem(shift + stride * q, 128), 1), total)
        sent[8 * r : 8 * r + 8, :] = total
    sent[64:80, :] = coefs[0:16, :]


def gather_blocks(spread, offsets, k, d):
    rows = []
    shift_one, shift_two = offsets[0, k], offsets[1, k]
    for at in (d + shift_one, d + shift_two, d + 8 - shift_one, d + 8 - shift_two):
        start = pl.multiple_of(512 * k + 64 * lax.rem(at, 8), 64)
        rows.append(spread[pl.ds(start, 64), :])
    return jnp.concatenate(rows, axis=0)


def again_kernel(columns_out, after, sent):
    sent[...] = columns_out[...]


def inner_kernel(first, slots, coefs, weights, offsets_at, *rest):
    out, faces, spread, offsets, arrived = rest[-5:]
    bi, bj = device_block(lax.axis_index("chaos"))
    before = (lax.axis_index("sx") == 0) & (bi == 0) & (bj > 0) & (bj < 7)

    @pl.when(before == first)
    def _():
        copy = pltpu.make_async_copy(offsets_at, offsets, arrived.at[0])
        copy.start()
        inner_operator(slots, coefs, weights, offsets, copy, out, faces, spread)


def inner_operator(slots, coefs, weights, offsets, offsets_copy, out, faces, spread):
    lane = lane_numbers()
    column = lane & 15
    even = lane & 1 == 0
    bi, bj = device_block(lax.axis_index("chaos"))
    top, bottom = lane < 16, lane >= 112
    left, right = column < 2, column >= 14
    left_half = column < 8
    unit_first, unit_second, unit_third = unit_masks(lane)
    row_edge = ((bi == 0) & top) | ((bi == 3) & bottom)
    column_edge = ((bj == 0) & left) | ((bj == 7) & right)

    def neighbours(block, beside, sides):
        return (
            jnp.where(top, beside, roll(block, 16)),
            jnp.where(bottom, beside, roll(block, -16)),
            jnp.where(left, sides, roll(block, 2)),
            jnp.where(right, sides, roll(block, -2)),
            jnp.where(even, roll(block, -1), roll(block, 1)),
        )

    for h in range(2):
        center = coefs[8 * h : 8 * h + 8, :]
        beside = coefs[16 + 8 * h : 24 + 8 * h, :]
        sides = coefs[32 + 8 * h : 40 + 8 * h, :]
        for face, other in enumerate(neighbours(center, beside, sides)):
            weight = (center + other) * 0.5
            for k in range(8 * h, min(8 * h + 8, MODES + 1)):
                faces[5 * k + face] = jnp.broadcast_to(weight[k - 8 * h : k - 8 * h + 1], (8, 128))

    def one_slot(s, carry):
        units = slots[s, 16:24, :]
        opened = jnp.where(unit_third, units, roll(units, 32))
        opened = jnp.where(unit_second, opened, roll(opened, 16))
        opened = jnp.where(unit_first, opened, roll(opened, 8))
        halves = []
        for h in range(2):
            block = slots[s, 8 * h : 8 * h + 8, :]
            beside = jnp.where(row_edge, block, roll(units, -(80 + 32 * h)))
            sides = jnp.where(left_half, roll(opened, -(16 + 4 * h)), roll(opened, 12 - 4 * h))
            sides = jnp.where(column_edge, block, sides)
            others = neighbours(block, beside, sides)
            halves.append((block, [block - other for other in others]))

        def diffuse(k):
            sums = []
            for block, steps in halves:
                total = faces[5 * k] * steps[0]
                for face in range(1, 5):
                    total = total + faces[5 * k + face] * steps[face]
                sums.append(total)
            return sums

        for h, total in enumerate(diffuse(0)):
            out[s, 8 * h : 8 * h + 8, :] = halves[h][0] + total
        for k in range(MODES):
            total = jnp.concatenate(diffuse(k + 1), axis=0)
            high = total.astype(bf16)
            low = (total - high.astype(f32)).astype(bf16)
            at = pl.ds(pl.multiple_of(512 * k + 16 * s, 16), 16)
            spread[at, 0:128] = high
            spread[at, 128:256] = low
        return carry

    lax.fori_loop(0, 32, one_slot, 0, unroll=8)
    offsets_copy.wait()

    def one_block(d, carry):
        total = jnp.zeros((64, 256), f32)
        for k in range(MODES):
            blocks = gather_blocks(spread, offsets, k, d)
            total = total + jnp.dot(weights[d, k], blocks, preferred_element_type=f32)
        mixed = total[:, :128] + total[:, 128:]
        for part in range(4):
            out[4 * d + part] = out[4 * d + part] + mixed[16 * part : 16 * part + 16]
        return carry

    lax.fori_loop(0, 8, one_block, 0, unroll=8)


def edge_kernel(rows_out, rows_in, columns_out, columns_first, columns_later, weights, offsets_at, inner, source, out, field, steps, spread, columns_in,
    offsets, arrived,
):
    bi, bj = device_block(lax.axis_index("chaos"))
    on_row = (bi == 0) | (bi == 3)
    on_column = (bj == 0) | (bj == 7)
    offsets_copy = pltpu.make_async_copy(offsets_at, offsets, arrived.at[0])
    offsets_copy.start()
    field_copy = pltpu.make_async_copy(source, field, arrived.at[1])
    field_copy.start()

    @pl.when(jnp.logical_not(on_row | on_column))
    def _():
        out[: 32 - FIRST] = inner[FIRST:]
        out[32 - FIRST :] = inner[:FIRST]
        offsets_copy.wait()

    early = lax.axis_index("sx") == 0

    @pl.when(on_column & early)
    def _():
        columns_in[...] = columns_first[...]

    @pl.when(jnp.logical_not(on_column & early))
    def _():
        columns_in[...] = columns_later[...]

    @pl.when(on_row | on_column)
    def _():
        edge_faces(
            bi, bj, on_row, on_column, rows_out, rows_in, columns_out, columns_in, weights, offsets, inner, out, steps, spread,
            offsets_copy,
        )

    field_copy.wait()


def edge_faces(
    bi, bj, on_row, on_column, rows_out, rows_in, columns_out, columns_in, weights, offsets, inner, out, steps, spread,
    offsets_copy,
):
    lane = lane_numbers()
    column = lane & 15
    for r in range(8):
        rows = slice(8 * r, 8 * r + 8)
        step = rows_out[rows, :] - rows_in[rows, :]
        for bit in (1, 2, 4):
            outer, inner_bit = lane & (16 * bit) != 0, lane & (2 * bit) != 0
            step = jnp.where(
                outer == inner_bit, step, jnp.where(outer, roll(step, 14 * bit), roll(step, -14 * bit))
            )
        steps[rows, :] = step
        steps[64 + 8 * r : 72 + 8 * r, :] = columns_out[rows, :] - columns_in[rows, :]
    row_own, row_other = jnp.where(bi == 0, 0, 16), jnp.where(bi == 0, 16, 0)
    column_own, column_other = jnp.where(bj == 0, 0, 114), jnp.where(bj == 0, 114, 0)
    row_share = jnp.where(on_row, 0.5, 0.0)
    column_share = jnp.where(on_column, 0.5, 0.0)
    factors = []
    for h in range(2):
        terms = slice(64 + 8 * h, 72 + 8 * h)
        row = pltpu.roll(rows_out[terms, :], row_own, 1) + pltpu.roll(rows_in[terms, :], row_other, 1)
        row = jnp.where(lane < 8, row, roll(row, 56))
        row = jnp.where(lane & 63 < 4, row, roll(row, 28))
        row = jnp.where(lane & 31 < 2, row, roll(row, 14))
        side = pltpu.roll(columns_out[terms, :], column_own, 1) + pltpu.roll(
            columns_in[terms, :], column_other, 1
        )
        row, side = row * row_share, side * column_share
        joined = jnp.where(column < 2, side, roll(side, 2))
        joined = jnp.where(column < 4, joined, jnp.where(column < 6, roll(row, 4), roll(row, 6)))
        factors.append(jnp.where(column < 8, joined, 0.0))
    wide_factors = [
        jnp.broadcast_to(factors[k // 8][k % 8 : k % 8 + 1, :], (8, 128)) for k in range(MODES + 1)
    ]
    low_part = column & 2 != 0
    first_two, first_four, first_six = column < 2, column < 4, column < 6

    def scaled(k, step):
        return wide_factors[k] * step

    for q in range(8):
        for r in range(4):
            halves = []
            for half in range(2):
                at = 8 * (2 * r + half)
                row, side = steps[at : at + 8, :], steps[64 + at : 72 + at, :]
                step = jnp.where(first_two, roll(side, -2 * q), roll(side, 2 - 2 * q))
                other = jnp.where(first_six, roll(row, 4 - 2 * q), roll(row, 6 - 2 * q))
                halves.append(jnp.where(first_four, step, other))
            at = 64 * q + 16 * r
            for k in range(MODES):
                parts = []
                for step in halves:
                    total = scaled(k + 1, step)
                    high = total.astype(bf16).astype(f32)
                    parts.append(jnp.where(low_part, total - high, total))
                spread[512 * k + at : 512 * k + at + 16, :] = jnp.concatenate(parts, axis=0).astype(bf16)
            for half, step in enumerate(halves):
                start = 128 + at + 8 * half
                steps[start : start + 8, :] = jnp.where(low_part, 0.0, scaled(0, step))
    from_lane = lax.broadcasted_iota(jnp.int32, (128, 128), 0)
    to_lane = lax.broadcasted_iota(jnp.int32, (128, 128), 1)
    from_column, from_row, plane = from_lane & 15, from_lane >> 4, from_lane & 1
    side_to = 16 * from_row + jnp.where(bj == 0, 0, 14) + plane
    row_to = jnp.where(bi == 0, 0, 112) + 2 * from_row + plane
    lands = jnp.where(from_column < 4, side_to, row_to)
    place = jnp.where((from_column < 8) & (lands == to_lane), 1.0, 0.0).astype(bf16)
    place = jnp.concatenate([place] * 3, axis=0)
    offsets_copy.wait()

    def one_block(d, carry):
        total = steps[pl.ds(pl.multiple_of(128 + 64 * d, 64), 64), :]
        for k in range(MODES):
            blocks = gather_blocks(spread, offsets, k, d)
            total = total + jnp.dot(weights[d, k], blocks, preferred_element_type=f32)
        high = total.astype(bf16)
        rest = total - high.astype(f32)
        middle = rest.astype(bf16)
        low = (rest - middle.astype(f32)).astype(bf16)
        placed = jnp.dot(jnp.concatenate([high, middle, low], axis=1), place, preferred_element_type=f32)
        to = lax.rem(4 * d + 32 - FIRST, 32)
        for part in range(4):
            out[to + part] = inner[4 * d + part] + placed[16 * part : 16 * part + 16]
        return carry

    lax.fori_loop(0, 8, one_block, 0, unroll=8)


def finish_kernel(field, slots, scales, target, out, left):
    low = chunk_masks(lane_numbers())
    field_scale, applied_scale = scales[0:8, :], scales[8:16, :]
    copies = []
    for bi in range(4):
        for h in range(2):
            terms = slice(8 * h, 8 * h + 8)
            rows = swap_chunks([slots[(block_device(bi, bj) - FIRST) % 32, terms, :] for bj in range(8)], low)
            for i in range(8):
                at = 8 * bi + i
                out[terms, at, :] = field_scale * field[terms, at, :] - applied_scale * rows[i]
        part = pl.ds(8 * bi, 8)
        copies.append(pltpu.make_async_copy(out.at[:, part, :], target.at[:, part, :], left.at[bi]))
        copies[-1].start()
    for copy in copies:
        copy.wait()


def from_hbm(array):
    return pltpu.with_memory_space_constraint(array, pltpu.HBM)


def in_any():
    return pl.BlockSpec(memory_space=pl.ANY)


def in_hbm():
    return pl.BlockSpec(memory_space=pltpu.HBM)


def in_vmem():
    return pl.BlockSpec(memory_space=pltpu.VMEM)


def in_smem():
    return pl.BlockSpec(memory_space=pltpu.SMEM)


def call(kernel, ins, outs, scratch=(), cost=None, limit=32, aliases=None, name=None, out_specs=None):
    return pl.pallas_call(
        kernel,
        out_shape=outs,
        in_specs=ins,
        out_specs=out_specs or jax.tree.map(lambda _: in_vmem(), outs),
        scratch_shapes=scratch,
        cost_estimate=cost,
        input_output_aliases=aliases or {},
        compiler_params=pltpu.CompilerParams(vmem_limit_bytes=limit * 2**20),
        name=name or kernel.__name__,
    )


def per_device(right_side, mean_coef, mode_coef, coupling, offsets, lower_bound, upper_bound):
    shape = jax.ShapeDtypeStruct
    slots = call(
        pack_kernel,
        [in_hbm()],
        pltpu.HBM((32, 24, 128), f32),
        [
            pltpu.VMEM((16, 32, 128), f32),
            pltpu.VMEM((32, 24, 128), f32),
            pltpu.SemaphoreType.DMA((4,)),
            pltpu.SemaphoreType.DMA((32,)),
        ],
        out_specs=in_hbm(),
        limit=32,
    )(from_hbm(right_side))
    held = lax.all_to_all(slots, "chaos", 0, 0, tiled=True)
    offsets = from_hbm(offsets.T)
    weights, coefs, scales = call(
        prepare_kernel,
        [in_hbm()] * 4 + [in_smem()] * 2,
        (pltpu.VMEM((8, MODES, 64, 256), bf16), pltpu.VMEM((48, 128), f32), pltpu.VMEM((16, 128), f32)),
        [
            pltpu.VMEM((16 * MODES, 4096), bf16),
            pltpu.VMEM((512 * MODES + 64, 128), f32),
            pltpu.VMEM((16, 32, 128), f32),
            pltpu.VMEM((8, 8, 128), f32),
            pltpu.SMEM((2, MODES), jnp.int32),
            pltpu.SemaphoreType.DMA((4,)),
        ],
        pl.CostEstimate(flops=2**27, bytes_accessed=2**22, transcendentals=0),
        limit=32,
    )(from_hbm(coupling.reshape(16 * MODES, 4096)), offsets, from_hbm(mean_coef), from_hbm(mode_coef), lower_bound, upper_bound)
    def index(device, sx, sy):
        return (device * 4 + sx % 4) * 4 + sy % 4

    row_pairs, early_pairs, late_pairs = [], [], []
    for sx in range(4):
        for sy in range(4):
            for bj in range(8):
                low, high = block_device(0, bj), block_device(3, bj)
                row_pairs.append((index(high, sx, sy), index(low, sx + 1, sy)))
                row_pairs.append((index(low, sx, sy), index(high, sx - 1, sy)))
            for bi in range(4):
                low, high = block_device(bi, 0), block_device(bi, 7)
                pairs = early_pairs if sx == 0 else late_pairs
                pairs.append((index(high, sx, sy), index(low, sx, sy + 1)))
                pairs.append((index(low, sx, sy), index(high, sx, sy - 1)))
    axes = ("chaos", "sx", "sy")
    message = shape((80, 128), f32)
    offsets_scratch = [pltpu.SMEM((2, MODES), jnp.int32), pltpu.SemaphoreType.DMA((1,))]
    scratch = [
        pltpu.VMEM((5 * MODES + 5, 8, 128), f32),
        pltpu.VMEM((512 * MODES, 256), bf16),
    ] + offsets_scratch
    inner_cost = pl.CostEstimate(flops=2**32, bytes_accessed=2**24, transcendentals=0)
    inner_shape = pltpu.VMEM((32, 16, 128), f32)
    columns_out = call(
        functools.partial(send_kernel, False), [in_vmem()] * 2 + [in_any()], message, name="send_columns"
    )(held, coefs, coefs)
    columns_first = lax.ppermute(columns_out, axes, early_pairs)
    inner = call(
        functools.partial(inner_kernel, True),
        [in_vmem()] * 3 + [in_hbm()] + [in_any()],
        inner_shape,
        scratch,
        inner_cost,
        name="inner_before",
    )(held, coefs, weights, offsets, columns_out)
    rows_out = call(
        functools.partial(send_kernel, True), [in_vmem()] * 2 + [in_any()], message, name="send_rows"
    )(held, coefs, inner)
    rows_in = lax.ppermute(rows_out, axes, row_pairs)
    columns_again = call(again_kernel, [in_vmem(), in_any()], message, name="send_again")(
        columns_out, rows_out
    )
    columns_later = lax.ppermute(columns_again, axes, late_pairs)
    inner = call(
        functools.partial(inner_kernel, False),
        [in_vmem()] * 3 + [in_hbm(), in_vmem()] + [in_any()] * 2,
        inner_shape,
        scratch,
        inner_cost,
        aliases={4: 0},
        name="inner_after",
    )(held, coefs, weights, offsets, inner, columns_again, columns_first)
    applied, field = call(
        edge_kernel,
        [in_vmem()] * 6 + [in_hbm(), in_vmem(), in_hbm()],
        (pltpu.VMEM((32, 16, 128), f32), pltpu.VMEM(right_side.shape, f32)),
        [
            pltpu.VMEM((128 + 512, 128), f32),
            pltpu.VMEM((512 * MODES, 128), bf16),
            pltpu.VMEM((80, 128), f32),
            pltpu.SMEM((2, MODES), jnp.int32),
            pltpu.SemaphoreType.DMA((2,)),
        ],
    )(
        rows_out, rows_in, columns_out, columns_first, columns_later, weights, offsets, inner, from_hbm(right_side)
    )
    turned = [[(FIRST + i) % 32 for i in range(32)]]
    returned = lax.all_to_all(applied, "chaos", 0, 0, tiled=True, axis_index_groups=turned)
    return call(
        finish_kernel,
        [in_vmem()] * 3,
        pltpu.HBM(right_side.shape, f32),
        [pltpu.VMEM(right_side.shape, f32), pltpu.SemaphoreType.DMA((4,))],
        out_specs=in_hbm(),
    )(field, returned, scales)


def solution(mesh):
    return jax.shard_map(
        per_device,
        mesh=mesh,
        in_specs=(P("chaos", "sx", "sy"), P("sx", "sy"), P(None, "sx", "sy"), P(), P(), P(), P()),
        out_specs=P("chaos", "sx", "sy"),
        check_vma=False,
    )
```

```python
import functools

import jax
import jax.numpy as jnp
from jax import lax
from jax.experimental import pallas as pl
from jax.experimental.pallas import tpu as pltpu
from jax.sharding import PartitionSpec as P

f32 = jnp.float32
bf16 = jnp.bfloat16
MODES = 10
OUTER = ((2, 2), (3, 2), (3, 1), (2, 0), (2, 3), (1, 1), (1, 2), (2, 1))
INNER = ((0, 2), (0, 1), (0, 0), (1, 0), (3, 0), (3, 3), (0, 3), (1, 3))


def block_device(bi, bj):
    x, y = (OUTER if bi in (0, 3) else INNER)[bj]
    return y * 8 + x * 2 + (0, 0, 1, 1)[bi]


def device_block(index):
    core, chip = index % 2, index // 2
    halves = []
    for half in range(2):
        bits = 0
        for outer, chips in ((1, OUTER), (0, INNER)):
            for bj, (x, y) in enumerate(chips):
                if (4 * y + x) // 8 == half:
                    bits |= (8 * outer + bj) << (4 * ((4 * y + x) % 8))
        halves.append(bits - 2**32 if bits >= 2**31 else bits)
    entry = (jnp.where(chip < 8, halves[0], halves[1]) >> (4 * (chip % 8))) & 15
    bi = jnp.where(entry >= 8, 3 * core, 1 + core)
    return bi, entry % 8


FIRST = block_device(0, 0)


def lane_numbers():
    return lax.broadcasted_iota(jnp.int32, (8, 128), 1)


def roll(value, shift):
    if isinstance(shift, int):
        shift = shift % 128
        if shift == 0:
            return value
    return pltpu.roll(value, shift, 1)


def chunk_masks(lane):
    return {step: lane & (16 * step) == 0 for step in (1, 2, 4)}


def swap_chunks(rows, low):
    rows = list(rows)
    for step in (1, 2, 4):
        for i in range(8):
            if i & step == 0:
                a, b = rows[i], rows[i + step]
                rows[i] = jnp.where(low[step], a, roll(b, 16 * step))
                rows[i + step] = jnp.where(low[step], roll(a, -16 * step), b)
    return rows


def unit_masks(lane):
    return lane & 31 < 8, lane & 63 < 16, lane < 32


def pack_kernel(source, target, field, slots, arrived, left):
    copies = [
        pltpu.make_async_copy(
            source.at[:, 8 * bi : 8 * bi + 8, :], field.at[:, 8 * bi : 8 * bi + 8, :], arrived.at[bi]
        )
        for bi in range(4)
    ]
    for copy in copies:
        copy.start()
    lane = lane_numbers()
    low = chunk_masks(lane)
    unit_first, unit_second, unit_third = unit_masks(lane)
    column = lane & 15
    upper, unit_half = column >= 8, column < 4
    first_half = lane < 64
    for copy in copies:
        copy.wait()
    leaving = []
    for bi in range(4):
        blocks, above, below = [], [], []
        for h in range(2):
            terms = slice(8 * h, 8 * h + 8)
            rows = [field[terms, 8 * bi + i, :] for i in range(8)]
            blocks.append(swap_chunks(rows, low))
            above.append(field[terms, 8 * bi - 1, :] if bi > 0 else rows[0])
            below.append(field[terms, 8 * bi + 8, :] if bi < 3 else rows[7])
        beside = [below[0], above[0], below[1], above[1]]
        for step in (1, 2):
            for i in range(4):
                if i & step == 0:
                    a, b = beside[i], beside[i + step]
                    beside[i] = jnp.where(low[step], a, roll(b, 16 * step))
                    beside[i + step] = jnp.where(low[step], roll(a, -16 * step), b)
        beside = [roll(row, 64) for row in beside] + beside
        for bj in range(8):
            at = block_device(bi, bj)
            units = []
            for h in range(2):
                slots[at, 8 * h : 8 * h + 8, :] = blocks[h][bj]
                side = jnp.where(upper, blocks[h][(bj - 1) % 8], blocks[h][(bj + 1) % 8])
                units.append(roll(side, 2 + 4 * h))
            row = jnp.where(unit_half, units[0], units[1])
            row = jnp.where(unit_first, row, roll(row, -8))
            row = jnp.where(unit_second, row, roll(row, -16))
            row = jnp.where(unit_third, row, roll(row, -32))
            slots[at, 16:24, :] = jnp.where(first_half, row, beside[bj])
    for part in range(8):
        at = slice(4 * part, 4 * part + 4)
        leaving.append(pltpu.make_async_copy(slots.at[at], target.at[at], left.at[part]))
        leaving[-1].start()
    for copy in leaving:
        copy.wait()


def prepare_kernel(
    coupling_at, offsets_at, mean_at, mode_at, lower_bound, upper_bound, weights, coefs, scales, coupling, pairs, tile,
    parts, offsets, arrived,
):
    copies = [
        pltpu.make_async_copy(mean_at, tile.at[0], arrived.at[0]),
        pltpu.make_async_copy(mode_at, tile.at[1 : MODES + 1], arrived.at[1]),
        pltpu.make_async_copy(coupling_at, coupling, arrived.at[2]),
        pltpu.make_async_copy(offsets_at, offsets, arrived.at[3]),
    ]
    for copy in copies:
        copy.start()
    tile[MODES + 1 :] = jnp.zeros((15 - MODES, 32, 128), f32)
    lane = lane_numbers()
    low = chunk_masks(lane)
    first = lane < 64
    left_half = lane & 15 < 8
    bi, bj = device_block(lax.axis_index("chaos"))
    copies[0].wait()
    copies[1].wait()
    for h in range(2):
        terms = slice(8 * h, 8 * h + 8)
        blocks = swap_chunks([tile[terms, 8 * bi + i, :] for i in range(8)], low)
        for j in range(8):
            parts[j] = blocks[j]
        coefs[8 * h : 8 * h + 8, :] = parts[bj]
        above = tile[terms, lax.rem(8 * bi + 31, 32), :]
        below = tile[terms, lax.rem(8 * bi + 8, 32), :]
        coefs[16 + 8 * h : 24 + 8 * h, :] = jnp.where(
            first,
            pltpu.roll(above, lax.rem(128 - 16 * bj, 128), 1),
            pltpu.roll(below, lax.rem(240 - 16 * bj, 128), 1),
        )
        coefs[32 + 8 * h : 40 + 8 * h, :] = jnp.where(
            left_half, roll(parts[lax.rem(bj + 7, 8)], -14), roll(parts[lax.rem(bj + 1, 8)], 14)
        )
    out_row = lax.broadcasted_iota(jnp.int32, (64, 128), 0)
    out_col = lax.broadcasted_iota(jnp.int32, (64, 128), 1)
    pick = jnp.where(out_col & 63 == out_row, 1.0, 0.0).astype(bf16)
    wide = out_col < 64
    lower_end = jnp.full((8, 128), lower_bound[0], f32)
    upper_end = jnp.full((8, 128), upper_bound[0], f32)
    middle = (upper_end + lower_end) * 0.5
    half_width = (upper_end - lower_end) * 0.5
    spread_ratio = middle / half_width
    factor_now = 1.0 / spread_ratio
    factor_next = 1.0 / (2.0 * spread_ratio - factor_now)
    residual_scale = 2.0 * factor_next / half_width
    field_scale = (1.0 + factor_next * factor_now) / middle + residual_scale
    applied_scale = residual_scale / middle
    scales[0:8, :] = field_scale
    scales[8:16, :] = applied_scale
    copies[3].wait()
    copies[2].wait()

    def one_mode(k, carry):
        base = pl.multiple_of(512 * k, 512)
        for m in range(32):
            both = coupling[pl.ds(pl.multiple_of(16 * k, 16), 16), 128 * m : 128 * m + 128].astype(f32)
            one, two = both[:8], both[8:]
            pairs[pl.ds(base + 2 * m, 8, 64), :] = jnp.where(first, one, roll(two, 64))
            pairs[pl.ds(base + 2 * m + 1, 8, 64), :] = jnp.where(first, roll(one, 64), two)
        shift_one, shift_two = offsets[0, k], offsets[1, k]
        for d in range(8):
            weights[d, k, :, 0:128] = pairs[pl.ds(base + 64 * d, 64), :].astype(bf16)
            from_one = lax.rem(d + 8 - shift_one, 8)
            from_two = lax.rem(d + 8 - shift_two, 8)
            one = pairs[pl.ds(pl.multiple_of(base + 64 * from_one, 64), 64), :]
            two = pairs[pl.ds(pl.multiple_of(base + 64 * from_two, 64), 64), :]
            stack = jnp.concatenate([jnp.where(wide, one, 0.0), jnp.where(wide, 0.0, two)], axis=0)
            turned = lax.dot_general(
                pick, stack.astype(bf16), (((1,), (1,)), ((), ())), preferred_element_type=f32
            )
            weights[d, k, :, 128:256] = turned.astype(bf16)
        return carry

    lax.fori_loop(0, MODES, one_mode, 0, unroll=5)


def send_kernel(along_rows, slots, coefs, *rest):
    lane = lane_numbers()
    bi, bj = device_block(lax.axis_index("chaos"))
    if along_rows:
        shift, stride, place = jnp.where(bi == 0, 0, 16), 16, lane >> 4
    else:
        shift, stride, place = jnp.where(bj == 0, 0, 114), 2, (lane & 15) >> 1
    sent = rest[-1]
    for r in range(8):
        total = jnp.zeros((8, 128), f32)
        for q in range(8):
            at, h = 4 * q + r // 2, r % 2
            block = slots[at, 8 * h : 8 * h + 8, :]
            total = jnp.where(place == q, pltpu.roll(block, lax.rem(shift + stride * q, 128), 1), total)
        sent[8 * r : 8 * r + 8, :] = total
    sent[64:80, :] = coefs[0:16, :]


def gather_blocks(spread, offsets, k, d):
    rows = []
    shift_one, shift_two = offsets[0, k], offsets[1, k]
    for at in (d + shift_one, d + shift_two, d + 8 - shift_one, d + 8 - shift_two):
        start = pl.multiple_of(512 * k + 64 * lax.rem(at, 8), 64)
        rows.append(spread[pl.ds(start, 64), :])
    return jnp.concatenate(rows, axis=0)


def again_kernel(columns_out, after, sent):
    sent[...] = columns_out[...]


def inner_kernel(first, slots, coefs, weights, offsets_at, *rest):
    out, faces, spread, offsets, arrived = rest[-5:]
    bi, bj = device_block(lax.axis_index("chaos"))
    before = (lax.axis_index("sx") == 0) & (bi == 0) & (bj > 0) & (bj < 7)

    @pl.when(before == first)
    def _():
        copy = pltpu.make_async_copy(offsets_at, offsets, arrived.at[0])
        copy.start()
        inner_operator(slots, coefs, weights, offsets, copy, out, faces, spread)


def inner_operator(slots, coefs, weights, offsets, offsets_copy, out, faces, spread):
    lane = lane_numbers()
    column = lane & 15
    even = lane & 1 == 0
    bi, bj = device_block(lax.axis_index("chaos"))
    top, bottom = lane < 16, lane >= 112
    left, right = column < 2, column >= 14
    left_half = column < 8
    unit_first, unit_second, unit_third = unit_masks(lane)
    row_edge = ((bi == 0) & top) | ((bi == 3) & bottom)
    column_edge = ((bj == 0) & left) | ((bj == 7) & right)

    def neighbours(block, beside, sides):
        return (
            jnp.where(top, beside, roll(block, 16)),
            jnp.where(bottom, beside, roll(block, -16)),
            jnp.where(left, sides, roll(block, 2)),
            jnp.where(right, sides, roll(block, -2)),
            jnp.where(even, roll(block, -1), roll(block, 1)),
        )

    for h in range(2):
        center = coefs[8 * h : 8 * h + 8, :]
        beside = coefs[16 + 8 * h : 24 + 8 * h, :]
        sides = coefs[32 + 8 * h : 40 + 8 * h, :]
        for face, other in enumerate(neighbours(center, beside, sides)):
            weight = (center + other) * 0.5
            for k in range(8 * h, min(8 * h + 8, MODES + 1)):
                faces[5 * k + face] = jnp.broadcast_to(weight[k - 8 * h : k - 8 * h + 1], (8, 128))

    def one_slot(s, carry):
        units = slots[s, 16:24, :]
        opened = jnp.where(unit_third, units, roll(units, 32))
        opened = jnp.where(unit_second, opened, roll(opened, 16))
        opened = jnp.where(unit_first, opened, roll(opened, 8))
        halves = []
        for h in range(2):
            block = slots[s, 8 * h : 8 * h + 8, :]
            beside = jnp.where(row_edge, block, roll(units, -(80 + 32 * h)))
            sides = jnp.where(left_half, roll(opened, -(16 + 4 * h)), roll(opened, 12 - 4 * h))
            sides = jnp.where(column_edge, block, sides)
            others = neighbours(block, beside, sides)
            halves.append((block, [block - other for other in others]))

        def diffuse(k):
            sums = []
            for block, steps in halves:
                total = faces[5 * k] * steps[0]
                for face in range(1, 5):
                    total = total + faces[5 * k + face] * steps[face]
                sums.append(total)
            return sums

        for h, total in enumerate(diffuse(0)):
            out[s, 8 * h : 8 * h + 8, :] = halves[h][0] + total
        for k in range(MODES):
            total = jnp.concatenate(diffuse(k + 1), axis=0)
            high = total.astype(bf16)
            low = (total - high.astype(f32)).astype(bf16)
            at = pl.ds(pl.multiple_of(512 * k + 16 * s, 16), 16)
            spread[at, 0:128] = high
            spread[at, 128:256] = low
        return carry

    lax.fori_loop(0, 32, one_slot, 0, unroll=8)
    offsets_copy.wait()

    def one_block(d, carry):
        total = jnp.zeros((64, 256), f32)
        for k in range(MODES):
            blocks = gather_blocks(spread, offsets, k, d)
            total = total + jnp.dot(weights[d, k], blocks, preferred_element_type=f32)
        mixed = total[:, :128] + total[:, 128:]
        for part in range(4):
            out[4 * d + part] = out[4 * d + part] + mixed[16 * part : 16 * part + 16]
        return carry

    lax.fori_loop(0, 8, one_block, 0, unroll=8)


def edge_kernel(rows_out, rows_in, columns_out, columns_first, columns_later, weights, offsets_at, inner, source, out, field, steps, spread, columns_in,
    offsets, arrived,
):
    bi, bj = device_block(lax.axis_index("chaos"))
    on_row = (bi == 0) | (bi == 3)
    on_column = (bj == 0) | (bj == 7)
    offsets_copy = pltpu.make_async_copy(offsets_at, offsets, arrived.at[0])
    offsets_copy.start()
    field_copy = pltpu.make_async_copy(source, field, arrived.at[1])
    field_copy.start()

    @pl.when(jnp.logical_not(on_row | on_column))
    def _():
        out[: 32 - FIRST] = inner[FIRST:]
        out[32 - FIRST :] = inner[:FIRST]
        offsets_copy.wait()

    early = lax.axis_index("sx") == 0

    @pl.when(on_column & early)
    def _():
        columns_in[...] = columns_first[...]

    @pl.when(jnp.logical_not(on_column & early))
    def _():
        columns_in[...] = columns_later[...]

    @pl.when(on_row | on_column)
    def _():
        edge_faces(
            bi, bj, on_row, on_column, rows_out, rows_in, columns_out, columns_in, weights, offsets, inner, out, steps, spread,
            offsets_copy,
        )

    field_copy.wait()


def edge_faces(
    bi, bj, on_row, on_column, rows_out, rows_in, columns_out, columns_in, weights, offsets, inner, out, steps, spread,
    offsets_copy,
):
    lane = lane_numbers()
    column = lane & 15
    for r in range(8):
        rows = slice(8 * r, 8 * r + 8)
        step = rows_out[rows, :] - rows_in[rows, :]
        for bit in (1, 2, 4):
            outer, inner_bit = lane & (16 * bit) != 0, lane & (2 * bit) != 0
            step = jnp.where(
                outer == inner_bit, step, jnp.where(outer, roll(step, 14 * bit), roll(step, -14 * bit))
            )
        steps[rows, :] = step
        steps[64 + 8 * r : 72 + 8 * r, :] = columns_out[rows, :] - columns_in[rows, :]
    row_own, row_other = jnp.where(bi == 0, 0, 16), jnp.where(bi == 0, 16, 0)
    column_own, column_other = jnp.where(bj == 0, 0, 114), jnp.where(bj == 0, 114, 0)
    row_share = jnp.where(on_row, 0.5, 0.0)
    column_share = jnp.where(on_column, 0.5, 0.0)
    factors = []
    for h in range(2):
        terms = slice(64 + 8 * h, 72 + 8 * h)
        row = pltpu.roll(rows_out[terms, :], row_own, 1) + pltpu.roll(rows_in[terms, :], row_other, 1)
        row = jnp.where(lane < 8, row, roll(row, 56))
        row = jnp.where(lane & 63 < 4, row, roll(row, 28))
        row = jnp.where(lane & 31 < 2, row, roll(row, 14))
        side = pltpu.roll(columns_out[terms, :], column_own, 1) + pltpu.roll(
            columns_in[terms, :], column_other, 1
        )
        row, side = row * row_share, side * column_share
        joined = jnp.where(column < 2, side, roll(side, 2))
        joined = jnp.where(column < 4, joined, jnp.where(column < 6, roll(row, 4), roll(row, 6)))
        factors.append(jnp.where(column < 8, joined, 0.0))
    wide_factors = [
        jnp.broadcast_to(factors[k // 8][k % 8 : k % 8 + 1, :], (8, 128)) for k in range(MODES + 1)
    ]
    low_part = column & 2 != 0
    first_two, first_four, first_six = column < 2, column < 4, column < 6

    def scaled(k, step):
        return wide_factors[k] * step

    for q in range(8):
        for r in range(4):
            halves = []
            for half in range(2):
                at = 8 * (2 * r + half)
                row, side = steps[at : at + 8, :], steps[64 + at : 72 + at, :]
                step = jnp.where(first_two, roll(side, -2 * q), roll(side, 2 - 2 * q))
                other = jnp.where(first_six, roll(row, 4 - 2 * q), roll(row, 6 - 2 * q))
                halves.append(jnp.where(first_four, step, other))
            at = 64 * q + 16 * r
            for k in range(MODES):
                parts = []
                for step in halves:
                    total = scaled(k + 1, step)
                    high = total.astype(bf16).astype(f32)
                    parts.append(jnp.where(low_part, total - high, total))
                spread[512 * k + at : 512 * k + at + 16, :] = jnp.concatenate(parts, axis=0).astype(bf16)
            for half, step in enumerate(halves):
                start = 128 + at + 8 * half
                steps[start : start + 8, :] = jnp.where(low_part, 0.0, scaled(0, step))
    from_lane = lax.broadcasted_iota(jnp.int32, (128, 128), 0)
    to_lane = lax.broadcasted_iota(jnp.int32, (128, 128), 1)
    from_column, from_row, plane = from_lane & 15, from_lane >> 4, from_lane & 1
    side_to = 16 * from_row + jnp.where(bj == 0, 0, 14) + plane
    row_to = jnp.where(bi == 0, 0, 112) + 2 * from_row + plane
    lands = jnp.where(from_column < 4, side_to, row_to)
    place = jnp.where((from_column < 8) & (lands == to_lane), 1.0, 0.0).astype(bf16)
    place = jnp.concatenate([place] * 3, axis=0)
    offsets_copy.wait()

    def one_block(d, carry):
        total = steps[pl.ds(pl.multiple_of(128 + 64 * d, 64), 64), :]
        for k in range(MODES):
            blocks = gather_blocks(spread, offsets, k, d)
            total = total + jnp.dot(weights[d, k], blocks, preferred_element_type=f32)
        high = total.astype(bf16)
        rest = total - high.astype(f32)
        middle = rest.astype(bf16)
        low = (rest - middle.astype(f32)).astype(bf16)
        placed = jnp.dot(jnp.concatenate([high, middle, low], axis=1), place, preferred_element_type=f32)
        to = lax.rem(4 * d + 32 - FIRST, 32)
        for part in range(4):
            out[to + part] = inner[4 * d + part] + placed[16 * part : 16 * part + 16]
        return carry

    lax.fori_loop(0, 8, one_block, 0, unroll=8)


def finish_kernel(field, slots, scales, target, out, left):
    low = chunk_masks(lane_numbers())
    field_scale, applied_scale = scales[0:8, :], scales[8:16, :]
    copies = []
    for bi in range(4):
        for h in range(2):
            terms = slice(8 * h, 8 * h + 8)
            rows = swap_chunks([slots[(block_device(bi, bj) - FIRST) % 32, terms, :] for bj in range(8)], low)
            for i in range(8):
                at = 8 * bi + i
                out[terms, at, :] = field_scale * field[terms, at, :] - applied_scale * rows[i]
        part = pl.ds(8 * bi, 8)
        copies.append(pltpu.make_async_copy(out.at[:, part, :], target.at[:, part, :], left.at[bi]))
        copies[-1].start()
    for copy in copies:
        copy.wait()


def from_hbm(array):
    return pltpu.with_memory_space_constraint(array, pltpu.HBM)


def in_any():
    return pl.BlockSpec(memory_space=pl.ANY)


def in_hbm():
    return pl.BlockSpec(memory_space=pltpu.HBM)


def in_vmem():
    return pl.BlockSpec(memory_space=pltpu.VMEM)


def in_smem():
    return pl.BlockSpec(memory_space=pltpu.SMEM)


def call(kernel, ins, outs, scratch=(), cost=None, limit=32, aliases=None, name=None, out_specs=None):
    return pl.pallas_call(
        kernel,
        out_shape=outs,
        in_specs=ins,
        out_specs=out_specs or jax.tree.map(lambda _: in_vmem(), outs),
        scratch_shapes=scratch,
        cost_estimate=cost,
        input_output_aliases=aliases or {},
        compiler_params=pltpu.CompilerParams(vmem_limit_bytes=limit * 2**20),
        name=name or kernel.__name__,
    )


def per_device(right_side, mean_coef, mode_coef, coupling, offsets, lower_bound, upper_bound):
    shape = jax.ShapeDtypeStruct
    slots = call(
        pack_kernel,
        [in_hbm()],
        pltpu.HBM((32, 24, 128), f32),
        [
            pltpu.VMEM((16, 32, 128), f32),
            pltpu.VMEM((32, 24, 128), f32),
            pltpu.SemaphoreType.DMA((4,)),
            pltpu.SemaphoreType.DMA((8,)),
        ],
        out_specs=in_hbm(),
        limit=32,
    )(from_hbm(right_side))
    held = lax.all_to_all(slots, "chaos", 0, 0, tiled=True)
    offsets = from_hbm(offsets.T)
    weights, coefs, scales = call(
        prepare_kernel,
        [in_hbm()] * 4 + [in_smem()] * 2,
        (pltpu.VMEM((8, MODES, 64, 256), bf16), pltpu.VMEM((48, 128), f32), pltpu.VMEM((16, 128), f32)),
        [
            pltpu.VMEM((16 * MODES, 4096), bf16),
            pltpu.VMEM((512 * MODES + 64, 128), f32),
            pltpu.VMEM((16, 32, 128), f32),
            pltpu.VMEM((8, 8, 128), f32),
            pltpu.SMEM((2, MODES), jnp.int32),
            pltpu.SemaphoreType.DMA((4,)),
        ],
        pl.CostEstimate(flops=2**27, bytes_accessed=2**22, transcendentals=0),
        limit=32,
    )(from_hbm(coupling.reshape(16 * MODES, 4096)), offsets, from_hbm(mean_coef), from_hbm(mode_coef), lower_bound, upper_bound)
    def index(device, sx, sy):
        return (device * 4 + sx % 4) * 4 + sy % 4

    row_pairs, early_pairs, late_pairs = [], [], []
    for sx in range(4):
        for sy in range(4):
            for bj in range(8):
                low, high = block_device(0, bj), block_device(3, bj)
                row_pairs.append((index(high, sx, sy), index(low, sx + 1, sy)))
                row_pairs.append((index(low, sx, sy), index(high, sx - 1, sy)))
            for bi in range(4):
                low, high = block_device(bi, 0), block_device(bi, 7)
                pairs = early_pairs if sx == 0 else late_pairs
                pairs.append((index(high, sx, sy), index(low, sx, sy + 1)))
                pairs.append((index(low, sx, sy), index(high, sx, sy - 1)))
    axes = ("chaos", "sx", "sy")
    message = shape((80, 128), f32)
    offsets_scratch = [pltpu.SMEM((2, MODES), jnp.int32), pltpu.SemaphoreType.DMA((1,))]
    scratch = [
        pltpu.VMEM((5 * MODES + 5, 8, 128), f32),
        pltpu.VMEM((512 * MODES, 256), bf16),
    ] + offsets_scratch
    inner_cost = pl.CostEstimate(flops=2**32, bytes_accessed=2**24, transcendentals=0)
    inner_shape = pltpu.VMEM((32, 16, 128), f32)
    columns_out = call(
        functools.partial(send_kernel, False), [in_vmem()] * 2 + [in_any()], message, name="send_columns"
    )(held, coefs, coefs)
    columns_first = lax.ppermute(columns_out, axes, early_pairs)
    inner = call(
        functools.partial(inner_kernel, True),
        [in_vmem()] * 3 + [in_hbm()] + [in_any()],
        inner_shape,
        scratch,
        inner_cost,
        name="inner_before",
    )(held, coefs, weights, offsets, columns_out)
    rows_out = call(
        functools.partial(send_kernel, True), [in_vmem()] * 2 + [in_any()], message, name="send_rows"
    )(held, coefs, inner)
    rows_in = lax.ppermute(rows_out, axes, row_pairs)
    columns_again = call(again_kernel, [in_vmem(), in_any()], message, name="send_again")(
        columns_out, rows_out
    )
    columns_later = lax.ppermute(columns_again, axes, late_pairs)
    inner = call(
        functools.partial(inner_kernel, False),
        [in_vmem()] * 3 + [in_hbm(), in_vmem()] + [in_any()] * 2,
        inner_shape,
        scratch,
        inner_cost,
        aliases={4: 0},
        name="inner_after",
    )(held, coefs, weights, offsets, inner, columns_again, columns_first)
    applied, field = call(
        edge_kernel,
        [in_vmem()] * 6 + [in_hbm(), in_vmem(), in_hbm()],
        (pltpu.VMEM((32, 16, 128), f32), pltpu.VMEM(right_side.shape, f32)),
        [
            pltpu.VMEM((128 + 512, 128), f32),
            pltpu.VMEM((512 * MODES, 128), bf16),
            pltpu.VMEM((80, 128), f32),
            pltpu.SMEM((2, MODES), jnp.int32),
            pltpu.SemaphoreType.DMA((2,)),
        ],
    )(
        rows_out, rows_in, columns_out, columns_first, columns_later, weights, offsets, inner, from_hbm(right_side)
    )
    turned = [[(FIRST + i) % 32 for i in range(32)]]
    returned = lax.all_to_all(applied, "chaos", 0, 0, tiled=True, axis_index_groups=turned)
    return call(
        finish_kernel,
        [in_vmem()] * 3,
        pltpu.HBM(right_side.shape, f32),
        [pltpu.VMEM(right_side.shape, f32), pltpu.SemaphoreType.DMA((4,))],
        out_specs=in_hbm(),
    )(field, returned, scales)


def solution(mesh):
    return jax.shard_map(
        per_device,
        mesh=mesh,
        in_specs=(P("chaos", "sx", "sy"), P("sx", "sy"), P(None, "sx", "sy"), P(), P(), P(), P()),
        out_specs=P("chaos", "sx", "sy"),
        check_vma=False,
    )
```
